256 devices in a mesh: blk: 64 (over z, x_lo, y), pair: 4 (over x_hi, core).
Axes of the slice: x: 4 (x_hi: 2, x_lo: 2; x = x_hi * 2 + x_lo), y: 4, z: 8, core: 2. Of those that a mesh axis runs over, the one named last changes fastest.
Arguments:
- points: float32 [8, 32768], P(None, ('blk', 'pair')), may hold values from -6 to 6
- lengthscale: float32 [8], replicated, may hold values from 0.8 to 4
- targets: float32 [8, 32768], P(None, ('blk', 'pair')), may hold values from -6 to 6
Outputs:
- residual: float32 [8, 32768], P(None, ('blk', 'pair'))
- direction: float32 [8, 32768], P(None, ('blk', 'pair'))
The draws below stay inside these ranges and needn't reach their ends.
All inputs are finite; a program needn't handle non-finite values.
Results may differ from the reference program's by a relative error of at most 0.0003.
Values sent between devices are 32-bit elements; how exact they have to be, the bound alone decides.
No kernel may reach another device: no remote copies, remote signals or barrier semaphores. Data moves between devices by JAX's collectives and lax.ppermute only.
A program may use at most 64 MiB of HBM per device.

```python
import math
import jax
import jax.numpy as jnp
from jax import lax

DIMS = 8
RHS = 8
ITERS = 2
NPTS = 32768


def shard_levels(stream_key, dims, pieces, least, top_value):
    gain = 1.0
    for position, shards_of in pieces:
        heights = jax.random.uniform(jax.random.fold_in(jax.random.fold_in(stream_key, 6), position), (shards_of,), jnp.float32, least / len(pieces), top_value / len(pieces))
        gain = gain * jnp.repeat(jnp.exp(heights), dims[position] // shards_of).reshape((-1,) + (1,) * (len(dims) - 1 - position))
    return gain


def noise(own_key, shape, spread, bound, split=(), held_as=jnp.bfloat16):
    array = spread * jax.random.normal(own_key, shape, jnp.float32)
    if split:
        array = array * shard_levels(own_key, shape, split, -0.22, 0.18)
    return jnp.clip(array, -bound, bound).astype(held_as)


def setup_inputs(seed: int = 0) -> dict:
    key_list = jax.random.split(jax.random.key(seed), 4)
    return {
        "points": noise(key_list[0], (DIMS, NPTS), 1.0, 6.0, ((1, 256),), jnp.float32),
        "lengthscale": jnp.clip(jnp.exp(jax.random.uniform(key_list[1], (DIMS,), jnp.float32, math.log(0.8), math.log(4.0))), 0.8, 4.0),
        "targets": noise(key_list[2], (RHS, NPTS), 1.0, 6.0, ((1, 256),), jnp.float32),
    }


root_five = math.sqrt(5.0)
noise_level = 0.5

def kernel_block(left_pts, left_square, right_pts, right_square):
    inner_part = jnp.dot(left_pts.T, right_pts, precision=lax.Precision.HIGHEST, preferred_element_type=jnp.float32)
    dist_square = jnp.maximum(left_square[:, None] + right_square[None, :] - 2.0 * inner_part, 0.0)
    scaled_dist = root_five * jnp.sqrt(dist_square)
    return (1.0 + scaled_dist + scaled_dist * scaled_dist / 3.0) * jnp.exp(-scaled_dist)

def reference(points, lengthscale, targets):
    scaled = points / lengthscale[:, None]
    sqnorm = lax.optimization_barrier(jnp.sum(scaled * scaled, axis=0))
    point_count = scaled.shape[1]
    block_size = math.gcd(point_count, 512)

    def operator_apply(values):

        def target_block(offset):
            rows_here = lax.dynamic_slice_in_dim(scaled, offset, block_size, 1)
            rows_square = lax.dynamic_slice_in_dim(sqnorm, offset, block_size, 0)
            kernel_tile = kernel_block(rows_here, rows_square, scaled, sqnorm)
            return jnp.dot(values, kernel_tile.T, precision=lax.Precision.HIGHEST, preferred_element_type=jnp.float32)
        offsets = jnp.arange(point_count // block_size, dtype=jnp.int32) * block_size
        blocks_out = lax.map(target_block, offsets)
        product = jnp.transpose(blocks_out, (1, 0, 2)).reshape(values.shape)
        return product + noise_level * values
    residual = targets
    direction = targets
    norm_now = lax.optimization_barrier(jnp.sum(residual * residual, axis=1))
    for iteration in range(ITERS):
        image_vec = operator_apply(direction)
        step_size = norm_now / lax.optimization_barrier(jnp.sum(direction * image_vec, axis=1))
        residual = residual - step_size[:, None] * image_vec
        norm_next = lax.optimization_barrier(jnp.sum(residual * residual, axis=1))
        direction = residual + (norm_next / norm_now)[:, None] * direction
        norm_now = norm_next
    return (residual, direction)
```

```python
import math

import jax
import jax.numpy as jnp
from jax import lax
from jax.experimental import pallas as pl
from jax.experimental.pallas import tpu as pltpu
from jax.sharding import Mesh
from jax.sharding import PartitionSpec as P

f32 = jnp.float32
bf16 = jnp.bfloat16
VMEM = pltpu.VMEM

AXES = ("z", "xl", "y", "xh", "core")
SIZES = (8, 2, 4, 2, 2)
ROWG = ("xl", "xh", "core")
COLG = ("z", "y")
NR, NC = 8, 32
OWN = 128
NI, NJ = NR * OWN, NC * OWN
noise_level = 0.5

POINT_SCALE = math.sqrt(5.0 / 3.0)
ROOT3 = math.sqrt(3.0)
EXP_SCALE = -math.sqrt(3.0) * math.log2(math.e)

TI, TJ = 256, 256


def pieces(x):
    first = x.astype(bf16).astype(f32)
    rest = x - first
    second = rest.astype(bf16).astype(f32)
    return first, second, rest - second


def features(x, left):
    x = x * POINT_SCALE
    square = jnp.sum(x * x, axis=0, keepdims=True)
    a, b, c = pieces(x)
    s1, s2, s3 = pieces(square)
    one, zero = jnp.ones_like(square), jnp.zeros_like(square)
    if left:
        tail = [s1, s2, s3, one, one, one, zero, zero]
        parts = [a, a, b, b, a, c]
    else:
        tail = [one, one, one, s1, s2, s3, zero, zero]
        parts = [-2.0 * a, -2.0 * b, -2.0 * a, -2.0 * b, -2.0 * c, -2.0 * a]
    return jnp.concatenate(parts + [jnp.concatenate(tail, 0), jnp.zeros_like(a)], 0)


def matern(tau):
    tau = jnp.maximum(tau, 1e-30)
    s = tau * lax.rsqrt(tau)
    return ((1.0 + tau) + ROOT3 * s) * jnp.exp2(EXP_SCALE * s)


def stacked(values):
    return jnp.concatenate(pieces(values), 0).astype(bf16)


def lanes(ref, first_row, count, start=0):
    return jnp.concatenate(
        [ref[start + k, first_row : first_row + 8, :] for k in range(count)], 1
    )


def total(x):
    return jnp.sum(x, axis=1, keepdims=True)


def first_product(rows_ref, cols_ref, high_ref, low_ref, out_ref):
    left = features(lanes(rows_ref, 0, NR), True).astype(bf16)
    right = features(lanes(cols_ref, 0, NC), False).T.astype(bf16)
    values = stacked(lanes(cols_ref, 8, NC))
    for i in range(0, NI, TI):
        acc = jnp.zeros((24, TI), f32)
        for j in range(0, NJ, TJ):
            tau = jnp.dot(right[j : j + TJ], left[:, i : i + TI], preferred_element_type=f32)
            tile = matern(tau)
            high = tile.astype(bf16)
            low = (tile - high.astype(f32)).astype(bf16)
            high_ref[j : j + TJ, i : i + TI] = high
            low_ref[j : j + TJ, i : i + TI] = low
            part = values[:, j : j + TJ]
            acc = acc + jnp.dot(part, high, preferred_element_type=f32)
            acc = acc + jnp.dot(part, low, preferred_element_type=f32)
        write_partial(out_ref, acc, i)


def write_partial(out_ref, acc, i):
    acc = acc[0:8] + acc[8:16] + acc[16:24]
    for k in range(TI // OWN):
        row = (i // OWN + k) * 8
        for copy in range(NR):
            out_ref[copy, row : row + 8, :] = acc[:, k * OWN : (k + 1) * OWN]


def block_rows(ref):
    out = []
    for k in range(NR):
        acc = ref[0, 8 * k : 8 * k + 8, :]
        for copy in range(1, NR):
            acc = acc + ref[copy, 8 * k : 8 * k + 8, :]
        out.append(acc)
    return out


def at_lanes(columns):
    lane = lax.broadcasted_iota(jnp.int32, (8, OWN), 1)
    out = jnp.zeros((8, OWN), f32)
    for k, column in enumerate(columns):
        out = jnp.where(lane == k, column, out)
    return out


def my_row_block():
    return lax.axis_index("xl") * 4 + lax.axis_index("xh") * 2 + lax.axis_index("core")


def first_image(mine_ref, part_ref, rows_ref, image_ref, out_ref):
    parts = block_rows(part_ref)
    bb = jnp.zeros((8, OWN), f32)
    bw = jnp.zeros((8, OWN), f32)
    for k in range(NR):
        target = rows_ref[k, 8:16, :]
        image = parts[k] + noise_level * target
        image_ref[k] = image
        bb = bb + target * target
        bw = bw + target * image
    own = image_ref[mine_ref[0]]
    scalars = at_lanes([total(bb), total(bw)])
    for copy in range(NC):
        out_ref[copy, 0:8, :] = own
        out_ref[copy, 8:16, :] = scalars


def second_product(cols_ref, image_cols_ref, high_ref, low_ref, out_ref, scalar_ref):
    sums = image_cols_ref[0, 8:16, :]
    for k in range(1, NC):
        sums = sums + image_cols_ref[k, 8:16, :]
    norm = sums[:, 0:1]
    step = norm / sums[:, 1:2]
    residual = lanes(cols_ref, 8, NC) - step * lanes(image_cols_ref, 0, NC)
    norm_part = total(residual * residual)
    values = stacked(residual)
    for i in range(0, NI, TI):
        acc = jnp.dot(values, high_ref[:, i : i + TI], preferred_element_type=f32)
        acc = acc + jnp.dot(values, low_ref[:, i : i + TI], preferred_element_type=f32)
        write_partial(out_ref, acc, i)
    for copy in range(NR):
        out_ref[copy, NI // OWN * 8 :, :] = jnp.broadcast_to(norm_part, (8, OWN))
    scalar_ref[...] = at_lanes([norm, step])


def second_image(mine_ref, part_ref, rows_ref, image_ref, scalar_ref, own_ref, out_ref, keep_ref):
    parts = block_rows(part_ref)
    norm, step = scalar_ref[:, 0:1], scalar_ref[:, 1:2]
    norm_next = part_ref[0, NI // OWN * 8 :, 0:1]
    for copy in range(1, NR):
        norm_next = norm_next + part_ref[copy, NI // OWN * 8 :, 0:1]
    ratio = norm_next / norm
    residuals, images = [], []
    di = jnp.zeros((8, OWN), f32)
    ri = jnp.zeros((8, OWN), f32)
    ii = jnp.zeros((8, OWN), f32)
    for k in range(NR):
        target = rows_ref[k, 8:16, :]
        image0 = image_ref[k]
        residual = target - step * image0
        direction = residual + ratio * target
        image = (parts[k] + noise_level * residual) + ratio * image0
        keep_ref[0, k] = residual
        keep_ref[1, k] = direction
        keep_ref[2, k] = image
        residuals.append(residual)
        images.append(image)
        di = di + direction * image
        ri = ri + residual * image
        ii = ii + image * image
    ii = total(ii)
    guess = total(ri) / jnp.where(ii > 0.0, ii, 1.0)
    ss = jnp.zeros((8, OWN), f32)
    si = jnp.zeros((8, OWN), f32)
    for k in range(NR):
        left = residuals[k] - guess * images[k]
        ss = ss + left * left
        si = si + left * images[k]
    scalars = at_lanes([total(di), guess, total(ss), total(si), ii])
    for copy in range(NC):
        out_ref[copy] = scalars
    own_ref[0] = keep_ref[0, mine_ref[0]]
    own_ref[1] = keep_ref[1, mine_ref[0]]
    own_ref[2] = keep_ref[2, mine_ref[0]]
    own_ref[3] = jnp.broadcast_to(norm_next, (8, OWN))


def finish(own_ref, sums_ref, residual_ref, direction_ref):
    norm = own_ref[3][:, 0:1]
    curvature = sums_ref[0][:, 0:1]
    for k in range(1, NC):
        curvature = curvature + sums_ref[k][:, 0:1]
    step = norm / curvature
    norm_next = jnp.zeros((8, 1), f32)
    for k in range(NC):
        block = sums_ref[k]
        off = step - block[:, 1:2]
        norm_next = norm_next + (block[:, 2:3] + off * (off * block[:, 4:5] - 2.0 * block[:, 3:4]))
    residual = own_ref[0] - step * own_ref[2]
    residual_ref[...] = residual
    direction_ref[...] = residual + (norm_next / norm) * own_ref[1]


def call(kernel, outs, name, args, scratch=(), vmem=48 << 20):
    return pl.pallas_call(
        kernel,
        in_specs=[
            pl.BlockSpec(memory_space=pltpu.SMEM if a.dtype == jnp.int32 else VMEM) for a in args
        ],
        out_specs=[pl.BlockSpec(memory_space=VMEM)] * len(outs),
        out_shape=outs,
        scratch_shapes=scratch,
        compiler_params=pltpu.CompilerParams(vmem_limit_bytes=vmem),
        name=name,
    )(*args)


def shape(*dims):
    return jax.ShapeDtypeStruct(dims, f32)


def per_device(points, lengthscale, targets):
    mine = my_row_block().astype(jnp.int32).reshape(1)
    own = jnp.concatenate([points / lengthscale[:, None], targets], 0)
    rows = lax.all_to_all(jnp.broadcast_to(own, (NR, 16, OWN)), ROWG, 0, 0)
    cols = lax.all_to_all(jnp.broadcast_to(own, (NC, 16, OWN)), COLG, 0, 0)
    tile = VMEM((NJ, NI), bf16)
    high, low, part = call(
        first_product, [tile, tile, shape(NR, NR * 8, OWN)], "first_product", [rows, cols], vmem=40 << 20
    )
    part = lax.all_to_all(part, ROWG, 0, 0)
    image, message = call(
        first_image, [shape(NR, 8, OWN), shape(NC, 16, OWN)], "first_image", [mine, part, rows]
    )
    image_cols = lax.all_to_all(message, COLG, 0, 0)
    high = pltpu.with_memory_space_constraint(high, VMEM)
    low = pltpu.with_memory_space_constraint(low, VMEM)
    part, scalars = call(
        second_product,
        [shape(NR, NR * 8 + 8, OWN), shape(8, OWN)],
        "second_product",
        [cols, image_cols, high, low],
        vmem=40 << 20,
    )
    part = lax.all_to_all(part, ROWG, 0, 0)
    keep, message = call(
        second_image,
        [shape(4, 8, OWN), shape(NC, 8, OWN)],
        "second_image",
        [mine, part, rows, image, scalars],
        scratch=[pltpu.VMEM((3, NR, 8, OWN), f32)],
    )
    sums = lax.all_to_all(message, COLG, 0, 0)
    residual, direction = call(
        finish, [shape(8, OWN), shape(8, OWN)], "finish", [keep, sums]
    )
    return residual, direction


def solution(mesh):
    fine = Mesh(mesh.devices.reshape(SIZES), AXES)
    placed = (P(None, AXES), P(), P(None, AXES))
    return jax.shard_map(
        per_device,
        mesh=fine,
        in_specs=placed,
        out_specs=(P(None, AXES), P(None, AXES)),
        check_vma=False,
    )
```

```python
import math

import jax
import jax.numpy as jnp
from jax import lax
from jax.experimental import pallas as pl
from jax.experimental.pallas import tpu as pltpu
from jax.sharding import Mesh
from jax.sharding import PartitionSpec as P

f32 = jnp.float32
bf16 = jnp.bfloat16
VMEM = pltpu.VMEM

AXES = ("z", "xl", "y", "xh", "core")
SIZES = (8, 2, 4, 2, 2)
ROWG = ("xl", "xh", "core")
COLG = ("z", "y")
NR, NC = 8, 32
OWN = 128
NI, NJ = NR * OWN, NC * OWN
noise_level = 0.5

POINT_SCALE = math.sqrt(5.0 / 3.0)
ROOT3 = math.sqrt(3.0)
EXP_SCALE = -math.sqrt(3.0) * math.log2(math.e)

TI, TJ = 256, 256


def pieces(x):
    first = x.astype(bf16).astype(f32)
    rest = x - first
    second = rest.astype(bf16).astype(f32)
    return first, second, rest - second


def features(x, left):
    x = x * POINT_SCALE
    square = jnp.sum(x * x, axis=0, keepdims=True)
    a, b, c = pieces(x)
    s1, s2, s3 = pieces(square)
    one, zero = jnp.ones_like(square), jnp.zeros_like(square)
    if left:
        tail = [s1, s2, s3, one, one, one, zero, zero]
        parts = [a, a, b, b, a, c]
    else:
        tail = [one, one, one, s1, s2, s3, zero, zero]
        parts = [-2.0 * a, -2.0 * b, -2.0 * a, -2.0 * b, -2.0 * c, -2.0 * a]
    return jnp.concatenate(parts + [jnp.concatenate(tail, 0), jnp.zeros_like(a)], 0)


def matern(tau):
    tau = jnp.maximum(tau, 1e-30)
    s = tau * lax.rsqrt(tau)
    return ((1.0 + tau) + ROOT3 * s) * jnp.exp2(EXP_SCALE * s)


def stacked(values):
    return jnp.concatenate(pieces(values), 0).astype(bf16)


def lanes(ref, first_row, count, start=0):
    return jnp.concatenate(
        [ref[start + k, first_row : first_row + 8, :] for k in range(count)], 1
    )


def total(x):
    return jnp.sum(x, axis=1, keepdims=True)


def first_product(rows_ref, cols_ref, high_ref, low_ref, out_ref):
    left = features(lanes(rows_ref, 0, NR), True).astype(bf16)
    right = features(lanes(cols_ref, 0, NC), False).T.astype(bf16)
    values = stacked(lanes(cols_ref, 8, NC))
    for i in range(0, NI, TI):
        acc = jnp.zeros((24, TI), f32)
        for j in range(0, NJ, TJ):
            tau = jnp.dot(right[j : j + TJ], left[:, i : i + TI], preferred_element_type=f32)
            tile = matern(tau)
            high = tile.astype(bf16)
            low = (tile - high.astype(f32)).astype(bf16)
            high_ref[j : j + TJ, i : i + TI] = high
            low_ref[j : j + TJ, i : i + TI] = low
            part = values[:, j : j + TJ]
            acc = acc + jnp.dot(part, high, preferred_element_type=f32)
            acc = acc + jnp.dot(part, low, preferred_element_type=f32)
        write_partial(out_ref, acc, i)


def write_partial(out_ref, acc, i):
    acc = acc[0:8] + acc[8:16] + acc[16:24]
    for k in range(TI // OWN):
        row = (i // OWN + k) * 8
        for copy in range(NR):
            out_ref[copy, row : row + 8, :] = acc[:, k * OWN : (k + 1) * OWN]


def block_rows(ref):
    out = []
    for k in range(NR):
        acc = ref[0, 8 * k : 8 * k + 8, :]
        for copy in range(1, NR):
            acc = acc + ref[copy, 8 * k : 8 * k + 8, :]
        out.append(acc)
    return out


def at_lanes(columns):
    lane = lax.broadcasted_iota(jnp.int32, (8, OWN), 1)
    out = jnp.zeros((8, OWN), f32)
    for k, column in enumerate(columns):
        out = jnp.where(lane == k, column, out)
    return out


def my_row_block():
    return lax.axis_index("xl") * 4 + lax.axis_index("xh") * 2 + lax.axis_index("core")


def first_image(part_ref, rows_ref, image_ref, out_ref):
    parts = block_rows(part_ref)
    bb = jnp.zeros((8, OWN), f32)
    bw = jnp.zeros((8, OWN), f32)
    for k in range(NR):
        target = rows_ref[k, 8:16, :]
        image = parts[k] + noise_level * target
        image_ref[k] = image
        bb = bb + target * target
        bw = bw + target * image
    own = image_ref[my_row_block()]
    scalars = at_lanes([total(bb), total(bw)])
    for copy in range(NC):
        out_ref[copy, 0:8, :] = own
        out_ref[copy, 8:16, :] = scalars


def second_product(cols_ref, image_cols_ref, high_ref, low_ref, out_ref, scalar_ref):
    sums = image_cols_ref[0, 8:16, :]
    for k in range(1, NC):
        sums = sums + image_cols_ref[k, 8:16, :]
    norm = sums[:, 0:1]
    step = norm / sums[:, 1:2]
    residual = lanes(cols_ref, 8, NC) - step * lanes(image_cols_ref, 0, NC)
    norm_part = total(residual * residual)
    values = stacked(residual)
    for i in range(0, NI, TI):
        acc = jnp.dot(values, high_ref[:, i : i + TI], preferred_element_type=f32)
        acc = acc + jnp.dot(values, low_ref[:, i : i + TI], preferred_element_type=f32)
        write_partial(out_ref, acc, i)
    for copy in range(NR):
        out_ref[copy, NI // OWN * 8 :, :] = jnp.broadcast_to(norm_part, (8, OWN))
    scalar_ref[...] = at_lanes([norm, step])


def second_image(part_ref, rows_ref, image_ref, scalar_ref, own_ref, out_ref, keep_ref):
    parts = block_rows(part_ref)
    norm, step = scalar_ref[:, 0:1], scalar_ref[:, 1:2]
    norm_next = part_ref[0, NI // OWN * 8 :, 0:1]
    for copy in range(1, NR):
        norm_next = norm_next + part_ref[copy, NI // OWN * 8 :, 0:1]
    ratio = norm_next / norm
    residuals, images = [], []
    di = jnp.zeros((8, OWN), f32)
    ri = jnp.zeros((8, OWN), f32)
    ii = jnp.zeros((8, OWN), f32)
    for k in range(NR):
        target = rows_ref[k, 8:16, :]
        image0 = image_ref[k]
        residual = target - step * image0
        direction = residual + ratio * target
        image = (parts[k] + noise_level * residual) + ratio * image0
        keep_ref[0, k] = residual
        keep_ref[1, k] = direction
        keep_ref[2, k] = image
        residuals.append(residual)
        images.append(image)
        di = di + direction * image
        ri = ri + residual * image
        ii = ii + image * image
    ii = total(ii)
    guess = total(ri) / jnp.where(ii > 0.0, ii, 1.0)
    ss = jnp.zeros((8, OWN), f32)
    si = jnp.zeros((8, OWN), f32)
    for k in range(NR):
        left = residuals[k] - guess * images[k]
        ss = ss + left * left
        si = si + left * images[k]
    scalars = at_lanes([total(di), guess, total(ss), total(si), ii])
    for copy in range(NC):
        out_ref[copy] = scalars
    mine = my_row_block()
    own_ref[0] = keep_ref[0, mine]
    own_ref[1] = keep_ref[1, mine]
    own_ref[2] = keep_ref[2, mine]
    own_ref[3] = jnp.broadcast_to(norm_next, (8, OWN))


def finish(own_ref, sums_ref, residual_ref, direction_ref):
    norm = own_ref[3][:, 0:1]
    curvature = sums_ref[0][:, 0:1]
    for k in range(1, NC):
        curvature = curvature + sums_ref[k][:, 0:1]
    step = norm / curvature
    norm_next = jnp.zeros((8, 1), f32)
    for k in range(NC):
        block = sums_ref[k]
        off = step - block[:, 1:2]
        norm_next = norm_next + (block[:, 2:3] + off * (off * block[:, 4:5] - 2.0 * block[:, 3:4]))
    residual = own_ref[0] - step * own_ref[2]
    residual_ref[...] = residual
    direction_ref[...] = residual + (norm_next / norm) * own_ref[1]


def call(kernel, outs, name, args, scratch=(), vmem=4 << 20):
    return pl.pallas_call(
        kernel,
        in_specs=[
            pl.BlockSpec(memory_space=VMEM) for _ in args
        ],
        out_specs=[pl.BlockSpec(memory_space=VMEM)] * len(outs),
        out_shape=outs,
        scratch_shapes=scratch,
        compiler_params=pltpu.CompilerParams(vmem_limit_bytes=vmem),
        name=name,
    )(*args)


def shape(*dims):
    return jax.ShapeDtypeStruct(dims, f32)


def per_device(points, lengthscale, targets):
    own = jnp.concatenate([points / lengthscale[:, None], targets], 0)
    rows = lax.all_to_all(jnp.broadcast_to(own, (NR, 16, OWN)), ROWG, 0, 0)
    cols = lax.all_to_all(jnp.broadcast_to(own, (NC, 16, OWN)), COLG, 0, 0)
    tile = VMEM((NJ, NI), bf16)
    high, low, part = call(
        first_product, [tile, tile, shape(NR, NR * 8, OWN)], "first_product", [rows, cols], vmem=24 << 20
    )
    part = lax.all_to_all(part, ROWG, 0, 0)
    image, message = call(
        first_image, [shape(NR, 8, OWN), shape(NC, 16, OWN)], "first_image", [part, rows]
    )
    image_cols = lax.all_to_all(message, COLG, 0, 0)
    high = pltpu.with_memory_space_constraint(high, VMEM)
    low = pltpu.with_memory_space_constraint(low, VMEM)
    part, scalars = call(
        second_product,
        [shape(NR, NR * 8 + 8, OWN), shape(8, OWN)],
        "second_product",
        [cols, image_cols, high, low],
        vmem=8 << 20,
    )
    part = lax.all_to_all(part, ROWG, 0, 0)
    keep, message = call(
        second_image,
        [shape(4, 8, OWN), shape(NC, 8, OWN)],
        "second_image",
        [part, rows, image, scalars],
        scratch=[pltpu.VMEM((3, NR, 8, OWN), f32)],
    )
    sums = lax.all_to_all(message, COLG, 0, 0)
    residual, direction = call(
        finish, [shape(8, OWN), shape(8, OWN)], "finish", [keep, sums]
    )
    return residual, direction


def solution(mesh):
    fine = Mesh(mesh.devices.reshape(SIZES), AXES)
    placed = (P(None, AXES), P(), P(None, AXES))
    return jax.shard_map(
        per_device,
        mesh=fine,
        in_specs=placed,
        out_specs=(P(None, AXES), P(None, AXES)),
        check_vma=False,
    )
```

```python
import math

import jax
import jax.numpy as jnp
from jax import lax
from jax.experimental import pallas as pl
from jax.experimental.pallas import tpu as pltpu
from jax.sharding import Mesh
from jax.sharding import PartitionSpec as P

f32 = jnp.float32
bf16 = jnp.bfloat16
VMEM = pltpu.VMEM

AXES = ("z", "xl", "y", "xh", "core")
SIZES = (8, 2, 4, 2, 2)
ROWG = ("xl", "xh", "core")
COLG = ("z", "y")
NR, NC = 8, 32
OWN = 128
NI, NJ = NR * OWN, NC * OWN
noise_level = 0.5

POINT_SCALE = math.sqrt(5.0 / 3.0)
ROOT3 = math.sqrt(3.0)
EXP_SCALE = -math.sqrt(3.0) * math.log2(math.e)

TI, TJ = 256, 256


def pieces(x):
    first = x.astype(bf16).astype(f32)
    rest = x - first
    second = rest.astype(bf16).astype(f32)
    return first, second, rest - second


def features(x, left):
    x = x * POINT_SCALE
    square = jnp.sum(x * x, axis=0, keepdims=True)
    a, b, c = pieces(x)
    s1, s2, s3 = pieces(square)
    one, zero = jnp.ones_like(square), jnp.zeros_like(square)
    if left:
        tail = [s1, s2, s3, one, one, one, zero, zero]
        parts = [a, a, b, b, a, c]
    else:
        tail = [one, one, one, s1, s2, s3, zero, zero]
        parts = [-2.0 * a, -2.0 * b, -2.0 * a, -2.0 * b, -2.0 * c, -2.0 * a]
    return jnp.concatenate(parts + [jnp.concatenate(tail, 0), jnp.zeros_like(a)], 0)


def matern(tau):
    tau = jnp.maximum(tau, 1e-30)
    s = tau * lax.rsqrt(tau)
    return ((1.0 + tau) + ROOT3 * s) * jnp.exp2(EXP_SCALE * s)


def stacked(values):
    return jnp.concatenate(pieces(values), 0).astype(bf16)


def lanes(ref, first_row, count, start=0):
    return jnp.concatenate(
        [ref[start + k, first_row : first_row + 8, :] for k in range(count)], 1
    )


def total(x):
    return jnp.sum(x, axis=1, keepdims=True)


def pack(points_hbm, lengthscale_hbm, targets_hbm, own_ref, copies_ref, points_ref, lengthscale_ref, targets_ref, sems):
    arriving = [
        pltpu.make_async_copy(points_hbm, points_ref, sems.at[0]),
        pltpu.make_async_copy(lengthscale_hbm, lengthscale_ref, sems.at[1]),
        pltpu.make_async_copy(targets_hbm, targets_ref, sems.at[2]),
    ]
    for copy in arriving:
        copy.start()
    for copy in arriving:
        copy.wait()
    row = lax.broadcasted_iota(jnp.int32, (8, OWN), 0)
    scale = jnp.zeros((8, OWN), f32)
    for k in range(8):
        scale = jnp.where(row == k, lengthscale_ref[k], scale)
    scaled = points_ref[...] / scale
    targets = targets_ref[...]
    own_ref[0, 0:8, :] = scaled
    own_ref[0, 8:16, :] = targets
    for copy in range(NC):
        copies_ref[copy, 0:8, :] = scaled
        copies_ref[copy, 8:16, :] = targets


def my_row_block():
    return lax.axis_index("xl") * 4 + lax.axis_index("xh") * 2 + lax.axis_index("core")


def first_product(rows_ref, cols_ref, high_ref, low_ref, out_ref):
    left = features(lanes(rows_ref, 0, NR), True).astype(bf16)
    right = features(lanes(cols_ref, 0, NC), False).T.astype(bf16)
    values = stacked(lanes(cols_ref, 8, NC))
    form = jnp.zeros((8, OWN), f32)
    for i in range(0, NI, TI):
        acc = jnp.zeros((24, TI), f32)
        for j in range(0, NJ, TJ):
            tau = jnp.dot(right[j : j + TJ], left[:, i : i + TI], preferred_element_type=f32)
            tile = matern(tau)
            high = tile.astype(bf16)
            low = (tile - high.astype(f32)).astype(bf16)
            high_ref[j : j + TJ, i : i + TI] = high
            low_ref[j : j + TJ, i : i + TI] = low
            part = values[:, j : j + TJ]
            acc = acc + jnp.dot(part, high, preferred_element_type=f32)
            acc = acc + jnp.dot(part, low, preferred_element_type=f32)
        acc = acc[0:8] + acc[8:16] + acc[16:24]
        for k in range(TI // OWN):
            block = i // OWN + k
            part = acc[:, k * OWN : (k + 1) * OWN]
            out_ref[block % 2, block // 2, 0:8, :] = part
            form = form + part * rows_ref[block, 8:16, :]
    form = jnp.broadcast_to(total(form), (8, OWN))
    for block in range(NR):
        out_ref[block % 2, block // 2, 8:16, :] = form


def at_lanes(columns):
    lane = lax.broadcasted_iota(jnp.int32, (8, OWN), 1)
    out = jnp.zeros((8, OWN), f32)
    for k, column in enumerate(columns):
        out = jnp.where(lane == k, column, out)
    return out


def first_image(own_ref, xh_ref, xl_ref, both_ref, rows_ref, out_ref):
    sums = (own_ref[0] + xh_ref[0]) + (xl_ref[0] + both_ref[0])
    targets = rows_ref[0, 8:16, :]
    bb = jnp.zeros((8, OWN), f32)
    for k in range(NR):
        bb = bb + rows_ref[k, 8:16, :] * rows_ref[k, 8:16, :]
    bb = total(bb)
    image = sums[0:8] + noise_level * targets
    scalars = at_lanes([bb, sums[8:16, 0:1] + noise_level * bb])
    for copy in range(NC):
        out_ref[copy, 0:8, :] = image
        out_ref[copy, 8:16, :] = scalars


def second_product(cols_ref, image_cols_ref, high_ref, low_ref, out_ref, image_ref, scalar_ref):
    sums = image_cols_ref[0, 8:16, :]
    for k in range(1, NC):
        sums = sums + image_cols_ref[k, 8:16, :]
    norm = sums[:, 0:1]
    step = norm / sums[:, 1:2]
    residual = lanes(cols_ref, 8, NC) - step * lanes(image_cols_ref, 0, NC)
    norm_part = jnp.broadcast_to(total(residual * residual), (8, OWN))
    values = stacked(residual)
    mine = my_row_block()
    image = image_cols_ref[my_col_block(), 0:8, :]
    for i in range(0, NI, TI):
        acc = jnp.dot(values, high_ref[:, i : i + TI], preferred_element_type=f32)
        acc = acc + jnp.dot(values, low_ref[:, i : i + TI], preferred_element_type=f32)
        acc = acc[0:8] + acc[8:16] + acc[16:24]
        for k in range(TI // OWN):
            row = pl.multiple_of((mine ^ (i // OWN + k)) * 8, 8)
            out_ref[pl.ds(row, 8), :] = acc[:, k * OWN : (k + 1) * OWN]
    out_ref[NR * 8 : NR * 8 + 8, :] = norm_part
    image_ref[...] = image
    scalar_ref[...] = at_lanes([norm, step])


def core_sum(ours_ref, theirs_ref, ours_image_ref, theirs_image_ref, out_ref):
    core = lax.axis_index("core")
    out_ref[0 : NR * 8 + 8, :] = ours_ref[...] + theirs_ref[...]
    first = pl.multiple_of(NR * 8 + 8 + core * 8, 8)
    out_ref[pl.ds(first, 8), :] = ours_image_ref[...]
    second = pl.multiple_of(NR * 8 + 16 - core * 8, 8)
    out_ref[pl.ds(second, 8), :] = theirs_image_ref[...]


def second_image(own_part, xh_part, xl_part, both_part, rows_ref, scalar_ref, own_ref, out_ref, keep_ref, part_ref):
    mine = my_row_block()
    chip = mine // 2
    for k, ref in enumerate((own_part, xh_part, xl_part, both_part)):
        part_ref[chip ^ k] = ref[...]
    norm, step = scalar_ref[:, 0:1], scalar_ref[:, 1:2]

    def summed(row):
        out = part_ref[0, row : row + 8, :]
        for k in range(1, 4):
            out = out + part_ref[k, row : row + 8, :]
        return out

    norm_next = summed(NR * 8)
    ratio = norm_next / norm
    residuals, images = [], []
    di = jnp.zeros((8, OWN), f32)
    ri = jnp.zeros((8, OWN), f32)
    ii = jnp.zeros((8, OWN), f32)
    for k in range(NR):
        target = rows_ref[mine ^ k, 8:16, :]
        first = NR * 8 + 8 + (k % 2) * 8
        image0 = part_ref[k // 2, first : first + 8, :]
        residual = target - step * image0
        direction = residual + ratio * target
        image = (summed(8 * k) + noise_level * residual) + ratio * image0
        keep_ref[0, k] = residual
        keep_ref[1, k] = direction
        keep_ref[2, k] = image
        residuals.append(residual)
        images.append(image)
        di = di + direction * image
        ri = ri + residual * image
        ii = ii + image * image
    ii = total(ii)
    guess = total(ri) / jnp.where(ii > 0.0, ii, 1.0)
    ss = jnp.zeros((8, OWN), f32)
    si = jnp.zeros((8, OWN), f32)
    for k in range(NR):
        left = residuals[k] - guess * images[k]
        ss = ss + left * left
        si = si + left * images[k]
    scalars = in_one_row([total(di), guess, total(ss), total(si), ii])
    for copy in range(NC):
        out_ref[copy] = scalars
    own_ref[0] = keep_ref[0, mine]
    own_ref[1] = keep_ref[1, mine]
    own_ref[2] = keep_ref[2, mine]
    own_ref[3] = norm_next


def in_one_row(columns):
    lane = lax.broadcasted_iota(jnp.int32, (8, OWN), 1)
    row = lax.broadcasted_iota(jnp.int32, (8, OWN), 0)
    out = jnp.zeros((8, OWN), f32)
    for k, column in enumerate(columns):
        out = jnp.where(lane == 8 * k + row, column, out)
    return jnp.sum(out, axis=0, keepdims=True)


def column_of(row_vector, k):
    lane = lax.broadcasted_iota(jnp.int32, (8, OWN), 1)
    row = lax.broadcasted_iota(jnp.int32, (8, OWN), 0)
    return total(jnp.where(lane == 8 * k + row, row_vector, 0.0))


def finish(own_ref, sums_ref, residual_ref, direction_ref):
    norm = own_ref[3][:, 0:1]
    rows = [sums_ref[k] for k in range(NC)]
    step = norm / column_of(sum(rows[1:], rows[0]), 0)
    norm_next = jnp.zeros((8, 1), f32)
    for k in range(NC):
        guess, ss, si, ii = [column_of(rows[k], q) for q in range(1, 5)]
        off = step - guess
        norm_next = norm_next + (ss + off * (off * ii - 2.0 * si))
    residual = own_ref[0] - step * own_ref[2]
    residual_ref[...] = residual
    direction_ref[...] = residual + (norm_next / norm) * own_ref[1]


def my_col_block():
    return lax.axis_index("z") * 4 + lax.axis_index("y")


def call(kernel, outs, name, args, scratch=(), vmem=4 << 20):
    return pl.pallas_call(
        kernel,
        in_specs=[
            pl.BlockSpec(memory_space=VMEM) for _ in args
        ],
        out_specs=[pl.BlockSpec(memory_space=VMEM)] * len(outs),
        out_shape=outs,
        scratch_shapes=scratch,
        compiler_params=pltpu.CompilerParams(vmem_limit_bytes=vmem),
        name=name,
    )(*args)


def shape(*dims):
    return jax.ShapeDtypeStruct(dims, f32)


def swap(x, axes):
    size = 2 ** len(axes)
    return lax.ppermute(x, axes, [(i, size - 1 - i) for i in range(size)])


CHIPS = (("xh",), ("xl",), ("xl", "xh"))


def per_device(points, lengthscale, targets):
    own, copies = pl.pallas_call(
        pack,
        in_specs=[pl.BlockSpec(memory_space=pltpu.HBM)] * 3,
        out_specs=[pl.BlockSpec(memory_space=VMEM)] * 2,
        out_shape=[shape(1, 16, OWN), shape(NC, 16, OWN)],
        scratch_shapes=[
            pltpu.VMEM((8, OWN), f32),
            pltpu.SMEM((8,), f32),
            pltpu.VMEM((8, OWN), f32),
            pltpu.SemaphoreType.DMA((3,)),
        ],
        compiler_params=pltpu.CompilerParams(vmem_limit_bytes=4 << 20),
        name="pack",
    )(*[pltpu.with_memory_space_constraint(a, pltpu.HBM) for a in (points, lengthscale, targets)])
    cols = lax.all_to_all(copies, COLG, 0, 0)
    rows = jnp.concatenate([own, swap(own, ("core",))], 0)
    rows = jnp.concatenate([rows] + [swap(rows, axes) for axes in CHIPS], 0)
    tile = VMEM((NJ, NI), bf16)
    high, low, part = call(
        first_product, [tile, tile, shape(2, 4, 16, OWN)], "first_product", [rows, cols], vmem=24 << 20
    )
    part = part[0] + swap(part[1], ("core",))
    parts = [part[0:1]] + [swap(part[k : k + 1], axes) for k, axes in enumerate(CHIPS, 1)]
    message = call(first_image, [shape(NC, 16, OWN)], "first_image", parts + [rows])[0]
    image_cols = lax.all_to_all(message, COLG, 0, 0)
    high = pltpu.with_memory_space_constraint(high, VMEM)
    low = pltpu.with_memory_space_constraint(low, VMEM)
    part, image, scalars = call(
        second_product,
        [shape(NR * 8 + 8, OWN), shape(8, OWN), shape(8, OWN)],
        "second_product",
        [cols, image_cols, high, low],
        vmem=8 << 20,
    )
    part = call(
        core_sum,
        [shape(NR * 8 + 24, OWN)],
        "core_sum",
        [part, swap(part, ("core",)), image, swap(image, ("core",))],
    )[0]
    parts = [part] + [swap(part, axes) for axes in CHIPS]
    keep, message = call(
        second_image,
        [shape(4, 8, OWN), shape(NC, 1, OWN)],
        "second_image",
        parts + [rows, scalars],
        scratch=[pltpu.VMEM((3, NR, 8, OWN), f32), pltpu.VMEM((4, NR * 8 + 24, OWN), f32)],
    )
    sums = lax.all_to_all(message, COLG, 0, 0)
    residual, direction = call(
        finish, [shape(8, OWN), shape(8, OWN)], "finish", [keep, sums]
    )
    return residual, direction


def solution(mesh):
    fine = Mesh(mesh.devices.reshape(SIZES), AXES)
    placed = (P(None, AXES), P(), P(None, AXES))
    return jax.shard_map(
        per_device,
        mesh=fine,
        in_specs=placed,
        out_specs=(P(None, AXES), P(None, AXES)),
        check_vma=False,
    )
```

```python
import math

import jax
import jax.numpy as jnp
from jax import lax
from jax.experimental import pallas as pl
from jax.experimental.pallas import tpu as pltpu
from jax.sharding import Mesh
from jax.sharding import PartitionSpec as P

f32 = jnp.float32
bf16 = jnp.bfloat16
VMEM = pltpu.VMEM

AXES = ("z", "xl", "y", "xh", "core")
SIZES = (8, 2, 4, 2, 2)
ROWG = ("xl", "xh", "core")
COLG = ("z", "y")
NR, NC = 8, 32
OWN = 128
NI, NJ = NR * OWN, NC * OWN
noise_level = 0.5

LOG2E = math.log2(math.e)
POINT_SCALE = math.sqrt(5.0) * LOG2E
SHIFT = 1.5 * LOG2E
REST = SHIFT * SHIFT / 3.0
FACTOR = 2.0**SHIFT * 0.75 / (SHIFT * SHIFT)

TI, TJ = 256, 256


def pieces(x):
    first = x.astype(bf16).astype(f32)
    rest = x - first
    second = rest.astype(bf16).astype(f32)
    return first, second, rest - second


def features(x, left):
    x = x * POINT_SCALE
    square = jnp.sum(x * x, axis=0, keepdims=True)
    a, b, c = pieces(x)
    s1, s2, s3 = pieces(square)
    one, zero = jnp.ones_like(square), jnp.zeros_like(square)
    if left:
        tail = [s1, s2, s3, one, one, one, zero, zero]
        parts = [a, a, b, b, a, c]
    else:
        tail = [one, one, one, s1, s2, s3, zero, zero]
        parts = [-2.0 * a, -2.0 * b, -2.0 * a, -2.0 * b, -2.0 * c, -2.0 * a]
    return jnp.concatenate(parts + [jnp.concatenate(tail, 0), jnp.zeros_like(a)], 0)


def matern(square):
    square = jnp.maximum(square, 1e-30)
    u = -SHIFT - square * lax.rsqrt(square)
    return (u * u + REST) * jnp.exp2(u)


def product(values, tile):
    high = tile.astype(bf16)
    low = (tile - high.astype(f32)).astype(bf16)
    out = jnp.dot(values, high, preferred_element_type=f32)
    return out + jnp.dot(values, low, preferred_element_type=f32)


def stacked(values):
    return jnp.concatenate(pieces(values), 0).astype(bf16)


def lanes(ref, first_row, count, start=0):
    return jnp.concatenate(
        [ref[start + k, first_row : first_row + 8, :] for k in range(count)], 1
    )


def total(x):
    return jnp.sum(x, axis=1, keepdims=True)


def pack(points_hbm, lengthscale_hbm, targets_hbm, own_ref, copies_ref, points_ref, lengthscale_ref, targets_ref, sems):
    arriving = [
        pltpu.make_async_copy(points_hbm, points_ref, sems.at[0]),
        pltpu.make_async_copy(lengthscale_hbm, lengthscale_ref, sems.at[1]),
        pltpu.make_async_copy(targets_hbm, targets_ref, sems.at[2]),
    ]
    for copy in arriving:
        copy.start()
    for copy in arriving:
        copy.wait()
    row = lax.broadcasted_iota(jnp.int32, (8, OWN), 0)
    scale = jnp.zeros((8, OWN), f32)
    for k in range(8):
        scale = jnp.where(row == k, lengthscale_ref[k], scale)
    scaled = points_ref[...] / scale
    targets = targets_ref[...]
    own_ref[0, 0:8, :] = scaled
    own_ref[0, 8:16, :] = targets
    for copy in range(NC):
        copies_ref[copy, 0:8, :] = scaled
        copies_ref[copy, 8:16, :] = targets


def my_row_block():
    return lax.axis_index("xl") * 4 + lax.axis_index("xh") * 2 + lax.axis_index("core")


def first_product(rows_ref, cols_ref, kernel_ref, out_ref):
    left = features(lanes(rows_ref, 0, NR), True).astype(bf16)
    right = features(lanes(cols_ref, 0, NC), False).T.astype(bf16)
    values = stacked(lanes(cols_ref, 8, NC))
    form = jnp.zeros((8, OWN), f32)
    for i in range(0, NI, TI):
        acc = jnp.zeros((24, TI), f32)
        for j in range(0, NJ, TJ):
            square = jnp.dot(right[j : j + TJ], left[:, i : i + TI], preferred_element_type=f32)
            tile = matern(square)
            kernel_ref[j : j + TJ, i : i + TI] = tile
            acc = acc + product(values[:, j : j + TJ], tile)
        acc = (acc[0:8] + acc[8:16] + acc[16:24]) * FACTOR
        for k in range(TI // OWN):
            block = i // OWN + k
            part = acc[:, k * OWN : (k + 1) * OWN]
            out_ref[block % 2, block // 2, 0:8, :] = part
            form = form + part * rows_ref[block, 8:16, :]
    form = jnp.broadcast_to(total(form), (8, OWN))
    for block in range(NR):
        out_ref[block % 2, block // 2, 8:16, :] = form


def at_lanes(columns):
    lane = lax.broadcasted_iota(jnp.int32, (8, OWN), 1)
    out = jnp.zeros((8, OWN), f32)
    for k, column in enumerate(columns):
        out = jnp.where(lane == k, column, out)
    return out


def first_image(own_ref, xh_ref, xl_ref, both_ref, rows_ref, out_ref, image_ref):
    sums = (own_ref[0] + xh_ref[0]) + (xl_ref[0] + both_ref[0])
    targets = rows_ref[0, 8:16, :]
    bb = jnp.zeros((8, OWN), f32)
    for k in range(NR):
        bb = bb + rows_ref[k, 8:16, :] * rows_ref[k, 8:16, :]
    bb = total(bb)
    image = sums[0:8] + noise_level * targets
    scalars = in_one_row([bb, sums[8:16, 0:1] + noise_level * bb])
    for copy in range(NC):
        for row in range(8):
            out_ref[9 * copy + row] = image[row : row + 1]
        out_ref[9 * copy + 8] = scalars
    image_ref[...] = image


def second_product(cols_ref, image_cols_ref, image_ref, kernel_ref, out_ref, scalar_ref):
    sums = image_cols_ref[8]
    for k in range(1, NC):
        sums = sums + image_cols_ref[9 * k + 8]
    norm = column_of(sums, 0)
    step = norm / column_of(sums, 1)
    images = [image_cols_ref[9 * k : 9 * k + 8].reshape(8, OWN) for k in range(NC)]
    residual = lanes(cols_ref, 8, NC) - step * jnp.concatenate(images, 1)
    norm_part = jnp.broadcast_to(total(residual * residual), (8, OWN))
    values = stacked(residual)
    mine = my_row_block()
    for i in range(0, NI, TI):
        acc = jnp.zeros((24, TI), f32)
        for j in range(0, NJ, TJ):
            acc = acc + product(values[:, j : j + TJ], kernel_ref[j : j + TJ, i : i + TI])
        acc = (acc[0:8] + acc[8:16] + acc[16:24]) * FACTOR
        for k in range(TI // OWN):
            row = pl.multiple_of((mine ^ (i // OWN + k)) * 8, 8)
            out_ref[pl.ds(row, 8), :] = acc[:, k * OWN : (k + 1) * OWN]
    out_ref[NR * 8 : NR * 8 + 8, :] = norm_part
    out_ref[NR * 8 + 8 :, :] = image_ref[...]
    scalar_ref[...] = at_lanes([norm, step])


def core_sum(ours_ref, theirs_ref, out_ref):
    core = lax.axis_index("core")
    sums = NR * 8 + 8
    out_ref[0:sums, :] = ours_ref[0:sums, :] + theirs_ref[0:sums, :]
    out_ref[pl.ds(pl.multiple_of(sums + core * 8, 8), 8), :] = ours_ref[sums:, :]
    out_ref[pl.ds(pl.multiple_of(sums + 8 - core * 8, 8), 8), :] = theirs_ref[sums:, :]


def second_image(own_part, xh_part, xl_part, both_part, rows_ref, scalar_ref, own_ref, out_ref, keep_ref, part_ref):
    mine = my_row_block()
    chip = mine // 2
    for k, ref in enumerate((own_part, xh_part, xl_part, both_part)):
        part_ref[chip ^ k] = ref[...]
    norm, step = scalar_ref[:, 0:1], scalar_ref[:, 1:2]

    def summed(row):
        out = part_ref[0, row : row + 8, :]
        for k in range(1, 4):
            out = out + part_ref[k, row : row + 8, :]
        return out

    norm_next = summed(NR * 8)
    ratio = norm_next / norm
    residuals, images = [], []
    di = jnp.zeros((8, OWN), f32)
    ri = jnp.zeros((8, OWN), f32)
    ii = jnp.zeros((8, OWN), f32)
    for k in range(NR):
        target = rows_ref[mine ^ k, 8:16, :]
        first = NR * 8 + 8 + (k % 2) * 8
        image0 = part_ref[k // 2, first : first + 8, :]
        residual = target - step * image0
        direction = residual + ratio * target
        image = (summed(8 * k) + noise_level * residual) + ratio * image0
        keep_ref[0, k] = residual
        keep_ref[1, k] = direction
        keep_ref[2, k] = image
        residuals.append(residual)
        images.append(image)
        di = di + direction * image
        ri = ri + residual * image
        ii = ii + image * image
    ii = total(ii)
    guess = total(ri) / jnp.where(ii > 0.0, ii, 1.0)
    ss = jnp.zeros((8, OWN), f32)
    si = jnp.zeros((8, OWN), f32)
    for k in range(NR):
        left = residuals[k] - guess * images[k]
        ss = ss + left * left
        si = si + left * images[k]
    scalars = in_one_row([total(di), guess, total(ss), total(si), ii])
    for copy in range(NC):
        out_ref[copy] = scalars
    own_ref[0] = keep_ref[0, mine]
    own_ref[1] = keep_ref[1, mine]
    own_ref[2] = keep_ref[2, mine]
    own_ref[3] = norm_next


def in_one_row(columns):
    lane = lax.broadcasted_iota(jnp.int32, (8, OWN), 1)
    row = lax.broadcasted_iota(jnp.int32, (8, OWN), 0)
    out = jnp.zeros((8, OWN), f32)
    for k, column in enumerate(columns):
        out = jnp.where(lane == 8 * k + row, column, out)
    return jnp.sum(out, axis=0, keepdims=True)


def column_of(row_vector, k):
    lane = lax.broadcasted_iota(jnp.int32, (8, OWN), 1)
    row = lax.broadcasted_iota(jnp.int32, (8, OWN), 0)
    return total(jnp.where(lane == 8 * k + row, row_vector, 0.0))


def finish(own_ref, sums_ref, residual_ref, direction_ref):
    norm = own_ref[3][:, 0:1]
    rows = [sums_ref[k] for k in range(NC)]
    step = norm / column_of(sum(rows[1:], rows[0]), 0)
    norm_next = jnp.zeros((8, 1), f32)
    for k in range(NC):
        guess, ss, si, ii = [column_of(rows[k], q) for q in range(1, 5)]
        off = step - guess
        norm_next = norm_next + (ss + off * (off * ii - 2.0 * si))
    residual = own_ref[0] - step * own_ref[2]
    residual_ref[...] = residual
    direction_ref[...] = residual + (norm_next / norm) * own_ref[1]


def call(kernel, outs, name, args, scratch=(), vmem=4 << 20):
    return pl.pallas_call(
        kernel,
        in_specs=[
            pl.BlockSpec(memory_space=VMEM) for _ in args
        ],
        out_specs=[pl.BlockSpec(memory_space=VMEM)] * len(outs),
        out_shape=outs,
        scratch_shapes=scratch,
        compiler_params=pltpu.CompilerParams(vmem_limit_bytes=vmem),
        name=name,
    )(*args)


def shape(*dims):
    return jax.ShapeDtypeStruct(dims, f32)


def swap(x, axes):
    size = 2 ** len(axes)
    return lax.ppermute(x, axes, [(i, size - 1 - i) for i in range(size)])


CHIPS = (("xh",), ("xl",), ("xl", "xh"))


def per_device(points, lengthscale, targets):
    own, copies = pl.pallas_call(
        pack,
        in_specs=[pl.BlockSpec(memory_space=pltpu.HBM)] * 3,
        out_specs=[pl.BlockSpec(memory_space=VMEM)] * 2,
        out_shape=[shape(1, 16, OWN), shape(NC, 16, OWN)],
        scratch_shapes=[
            pltpu.VMEM((8, OWN), f32),
            pltpu.SMEM((8,), f32),
            pltpu.VMEM((8, OWN), f32),
            pltpu.SemaphoreType.DMA((3,)),
        ],
        compiler_params=pltpu.CompilerParams(vmem_limit_bytes=4 << 20),
        name="pack",
    )(*[pltpu.with_memory_space_constraint(a, pltpu.HBM) for a in (points, lengthscale, targets)])
    cols = lax.all_to_all(copies, COLG, 0, 0)
    rows = jnp.concatenate([own, swap(own, ("core",))], 0)
    rows = jnp.concatenate([rows] + [swap(rows, axes) for axes in CHIPS], 0)
    kernel, part = call(
        first_product,
        [VMEM((NJ, NI), f32), shape(2, 4, 16, OWN)],
        "first_product",
        [rows, cols],
        vmem=24 << 20,
    )
    part = part[0] + swap(part[1], ("core",))
    parts = [part[0:1]] + [swap(part[k : k + 1], axes) for k, axes in enumerate(CHIPS, 1)]
    message, image = call(
        first_image, [shape(NC * 9, 1, OWN), shape(8, OWN)], "first_image", parts + [rows]
    )
    image_cols = lax.all_to_all(message, COLG, 0, 0, tiled=True)
    kernel = pltpu.with_memory_space_constraint(kernel, VMEM)
    part, scalars = call(
        second_product,
        [shape(NR * 8 + 16, OWN), shape(8, OWN)],
        "second_product",
        [cols, image_cols, image, kernel],
        vmem=8 << 20,
    )
    part = call(
        core_sum, [shape(NR * 8 + 24, OWN)], "core_sum", [part, swap(part, ("core",))]
    )[0]
    parts = [part] + [swap(part, axes) for axes in CHIPS]
    keep, message = call(
        second_image,
        [shape(4, 8, OWN), shape(NC, 1, OWN)],
        "second_image",
        parts + [rows, scalars],
        scratch=[pltpu.VMEM((3, NR, 8, OWN), f32), pltpu.VMEM((4, NR * 8 + 24, OWN), f32)],
    )
    sums = lax.all_to_all(message, COLG, 0, 0)
    residual, direction = call(
        finish, [shape(8, OWN), shape(8, OWN)], "finish", [keep, sums]
    )
    return residual, direction


def solution(mesh):
    fine = Mesh(mesh.devices.reshape(SIZES), AXES)
    placed = (P(None, AXES), P(), P(None, AXES))
    return jax.shard_map(
        per_device,
        mesh=fine,
        in_specs=placed,
        out_specs=(P(None, AXES), P(None, AXES)),
        check_vma=False,
    )
```

```python
import math

import jax
import jax.numpy as jnp
from jax import lax
from jax.experimental import pallas as pl
from jax.experimental.pallas import tpu as pltpu
from jax.sharding import Mesh
from jax.sharding import PartitionSpec as P

f32 = jnp.float32
bf16 = jnp.bfloat16
VMEM = pltpu.VMEM

AXES = ("z", "xl", "y", "xh", "core")
SIZES = (8, 2, 4, 2, 2)
NR, NC = 8, 32
OWN = 128
NI, NJ = NR * OWN, NC * OWN
noise_level = 0.5

LOG2E = math.log2(math.e)
POINT_SCALE = math.sqrt(5.0) * LOG2E
SHIFT = 1.5 * LOG2E
REST = SHIFT * SHIFT / 3.0
FACTOR = 2.0**SHIFT * 0.75 / (SHIFT * SHIFT)

TI, TJ = 256, 256


def pieces(x):
    first = x.astype(bf16).astype(f32)
    rest = x - first
    second = rest.astype(bf16).astype(f32)
    return first, second, rest - second


def features(x, left):
    x = x * POINT_SCALE
    square = jnp.sum(x * x, axis=0, keepdims=True)
    a, b, c = pieces(x)
    s1, s2, s3 = pieces(square)
    one, zero = jnp.ones_like(square), jnp.zeros_like(square)
    if left:
        tail = [s1, s2, s3, one, one, one, zero, zero]
        parts = [a, a, b, b, a, c]
    else:
        tail = [one, one, one, s1, s2, s3, zero, zero]
        parts = [-2.0 * a, -2.0 * b, -2.0 * a, -2.0 * b, -2.0 * c, -2.0 * a]
    return jnp.concatenate(parts + [jnp.concatenate(tail, 0), jnp.zeros_like(a)], 0)


def matern(square):
    square = jnp.maximum(square, 1e-30)
    u = -SHIFT - square * lax.rsqrt(square)
    return (u * u + REST) * jnp.exp2(u)


def product(values, tile):
    high = tile.astype(bf16)
    low = (tile - high.astype(f32)).astype(bf16)
    out = jnp.dot(values, high, preferred_element_type=f32)
    return out + jnp.dot(values, low, preferred_element_type=f32)


def stacked(values):
    return jnp.concatenate(pieces(values), 0).astype(bf16)


def lanes(ref, first_row, count, start=0):
    return jnp.concatenate(
        [ref[start + k, first_row : first_row + 8, :] for k in range(count)], 1
    )


def total(x):
    return jnp.sum(x, axis=1, keepdims=True)


def pack(points_hbm, lengthscale_hbm, targets_hbm, own_ref, copies_ref, points_ref, lengthscale_ref, targets_ref, sems):
    arriving = [
        pltpu.make_async_copy(points_hbm, points_ref, sems.at[0]),
        pltpu.make_async_copy(lengthscale_hbm, lengthscale_ref, sems.at[1]),
        pltpu.make_async_copy(targets_hbm, targets_ref, sems.at[2]),
    ]
    for copy in arriving:
        copy.start()
    for copy in arriving:
        copy.wait()
    row = lax.broadcasted_iota(jnp.int32, (8, OWN), 0)
    scale = jnp.zeros((8, OWN), f32)
    for k in range(8):
        scale = jnp.where(row == k, lengthscale_ref[k], scale)
    scaled = points_ref[...] / scale
    targets = targets_ref[...]
    own_ref[0, 0:8, :] = scaled
    own_ref[0, 8:16, :] = targets
    for copy in range(NC):
        copies_ref[copy, 0:8, :] = scaled
        copies_ref[copy, 8:16, :] = targets


def my_row_block():
    return lax.axis_index("xl") * 4 + lax.axis_index("xh") * 2 + lax.axis_index("core")


def first_product(rows_ref, cols_ref, kernel_ref, out_ref):
    left = features(lanes(rows_ref, 0, NR), True).astype(bf16)
    right = features(lanes(cols_ref, 0, NC), False).T.astype(bf16)
    values = stacked(lanes(cols_ref, 8, NC))
    form = jnp.zeros((8, OWN), f32)
    for i in range(0, NI, TI):
        acc = jnp.zeros((24, TI), f32)
        lag = TJ
        for j in range(0, NJ, TJ):
            square = jnp.dot(right[j : j + TJ], left[:, i : i + TI], preferred_element_type=f32)
            tile = matern(square)
            kernel_ref[j : j + TJ, i : i + TI] = tile
            if j >= lag:
                acc = acc + product(values[:, j - lag : j - lag + TJ], kernel_ref[j - lag : j - lag + TJ, i : i + TI])
        acc = acc + product(values[:, NJ - lag :], kernel_ref[NJ - lag :, i : i + TI])
        acc = (acc[0:8] + acc[8:16] + acc[16:24]) * FACTOR
        for k in range(TI // OWN):
            block = i // OWN + k
            part = acc[:, k * OWN : (k + 1) * OWN]
            out_ref[block % 2, block // 2, 0:8, :] = part
            form = form + part * rows_ref[block, 8:16, :]
    form = jnp.broadcast_to(total(form), (8, OWN))
    for block in range(NR):
        out_ref[block % 2, block // 2, 8:16, :] = form


def at_lanes(columns):
    lane = lax.broadcasted_iota(jnp.int32, (8, OWN), 1)
    out = jnp.zeros((8, OWN), f32)
    for k, column in enumerate(columns):
        out = jnp.where(lane == k, column, out)
    return out


def first_image(own_ref, xh_ref, xl_ref, both_ref, rows_ref, out_ref, image_ref):
    sums = (own_ref[0] + xh_ref[0]) + (xl_ref[0] + both_ref[0])
    targets = rows_ref[0, 8:16, :]
    bb = jnp.zeros((8, OWN), f32)
    for k in range(NR):
        bb = bb + rows_ref[k, 8:16, :] * rows_ref[k, 8:16, :]
    bb = total(bb)
    image = sums[0:8] + noise_level * targets
    scalars = in_one_row([bb, sums[8:16, 0:1] + noise_level * bb])
    for copy in range(NC):
        for row in range(8):
            out_ref[9 * copy + row] = image[row : row + 1]
        out_ref[9 * copy + 8] = scalars
    image_ref[...] = image


def second_product(cols_ref, image_cols_ref, image_ref, kernel_ref, out_ref, scalar_ref):
    sums = image_cols_ref[8]
    for k in range(1, NC):
        sums = sums + image_cols_ref[9 * k + 8]
    norm = column_of(sums, 0)
    step = norm / column_of(sums, 1)
    images = [image_cols_ref[9 * k : 9 * k + 8].reshape(8, OWN) for k in range(NC)]
    residual = lanes(cols_ref, 8, NC) - step * jnp.concatenate(images, 1)
    norm_part = jnp.broadcast_to(total(residual * residual), (8, OWN))
    values = stacked(residual)
    mine = my_row_block()
    for i in range(0, NI, TI):
        acc = jnp.zeros((24, TI), f32)
        for j in range(0, NJ, TJ):
            acc = acc + product(values[:, j : j + TJ], kernel_ref[j : j + TJ, i : i + TI])
        acc = (acc[0:8] + acc[8:16] + acc[16:24]) * FACTOR
        for k in range(TI // OWN):
            row = pl.multiple_of((mine ^ (i // OWN + k)) * 8, 8)
            out_ref[pl.ds(row, 8), :] = acc[:, k * OWN : (k + 1) * OWN]
    out_ref[NR * 8 : NR * 8 + 8, :] = norm_part
    out_ref[NR * 8 + 8 :, :] = image_ref[...]
    scalar_ref[...] = at_lanes([norm, step])


def core_sum(ours_ref, theirs_ref, out_ref):
    core = lax.axis_index("core")
    sums = NR * 8 + 8
    out_ref[0:sums, :] = ours_ref[0:sums, :] + theirs_ref[0:sums, :]
    out_ref[pl.ds(pl.multiple_of(sums + core * 8, 8), 8), :] = ours_ref[sums:, :]
    out_ref[pl.ds(pl.multiple_of(sums + 8 - core * 8, 8), 8), :] = theirs_ref[sums:, :]


def second_image(own_part, xh_part, xl_part, both_part, rows_ref, scalar_ref, own_ref, out_ref, keep_ref, part_ref):
    mine = my_row_block()
    chip = mine // 2
    for k, ref in enumerate((own_part, xh_part, xl_part, both_part)):
        part_ref[chip ^ k] = ref[...]
    norm, step = scalar_ref[:, 0:1], scalar_ref[:, 1:2]

    def summed(row):
        out = part_ref[0, row : row + 8, :]
        for k in range(1, 4):
            out = out + part_ref[k, row : row + 8, :]
        return out

    norm_next = summed(NR * 8)
    ratio = norm_next / norm
    residuals, images = [], []
    di = jnp.zeros((8, OWN), f32)
    ri = jnp.zeros((8, OWN), f32)
    ii = jnp.zeros((8, OWN), f32)
    for k in range(NR):
        target = rows_ref[mine ^ k, 8:16, :]
        first = NR * 8 + 8 + (k % 2) * 8
        image0 = part_ref[k // 2, first : first + 8, :]
        residual = target - step * image0
        direction = residual + ratio * target
        image = (summed(8 * k) + noise_level * residual) + ratio * image0
        keep_ref[0, k] = residual
        keep_ref[1, k] = direction
        keep_ref[2, k] = image
        residuals.append(residual)
        images.append(image)
        di = di + direction * image
        ri = ri + residual * image
        ii = ii + image * image
    ii = total(ii)
    guess = total(ri) / jnp.where(ii > 0.0, ii, 1.0)
    ss = jnp.zeros((8, OWN), f32)
    si = jnp.zeros((8, OWN), f32)
    for k in range(NR):
        left = residuals[k] - guess * images[k]
        ss = ss + left * left
        si = si + left * images[k]
    scalars = in_one_row([total(di), guess, total(ss), total(si), ii])
    for copy in range(NC):
        out_ref[copy] = scalars
    own_ref[0] = keep_ref[0, mine]
    own_ref[1] = keep_ref[1, mine]
    own_ref[2] = keep_ref[2, mine]
    own_ref[3] = norm_next


def in_one_row(columns):
    lane = lax.broadcasted_iota(jnp.int32, (8, OWN), 1)
    row = lax.broadcasted_iota(jnp.int32, (8, OWN), 0)
    out = jnp.zeros((8, OWN), f32)
    for k, column in enumerate(columns):
        out = jnp.where(lane == 8 * k + row, column, out)
    return jnp.sum(out, axis=0, keepdims=True)


def column_of(row_vector, k):
    lane = lax.broadcasted_iota(jnp.int32, (8, OWN), 1)
    row = lax.broadcasted_iota(jnp.int32, (8, OWN), 0)
    return total(jnp.where(lane == 8 * k + row, row_vector, 0.0))


def finish(own_ref, sums_ref, residual_ref, direction_ref):
    norm = own_ref[3][:, 0:1]
    rows = [sums_ref[k] for k in range(NC)]
    step = norm / column_of(sum(rows[1:], rows[0]), 0)
    norm_next = jnp.zeros((8, 1), f32)
    for k in range(NC):
        guess, ss, si, ii = [column_of(rows[k], q) for q in range(1, 5)]
        off = step - guess
        norm_next = norm_next + (ss + off * (off * ii - 2.0 * si))
    residual = own_ref[0] - step * own_ref[2]
    residual_ref[...] = residual
    direction_ref[...] = residual + (norm_next / norm) * own_ref[1]


def call(kernel, outs, name, args, scratch=(), vmem=4 << 20):
    return pl.pallas_call(
        kernel,
        in_specs=[
            pl.BlockSpec(memory_space=VMEM) for _ in args
        ],
        out_specs=[pl.BlockSpec(memory_space=VMEM)] * len(outs),
        out_shape=outs,
        scratch_shapes=scratch,
        compiler_params=pltpu.CompilerParams(vmem_limit_bytes=vmem),
        name=name,
    )(*args)


def shape(*dims):
    return jax.ShapeDtypeStruct(dims, f32)


def column_groups():
    order = [
        ((z + 4) % 8, ((y if z % 2 == 0 else 3 - y) + 2) % 4) for z in range(8) for y in range(4)
    ]
    return [
        [(((z * 2 + r // 4) * 4 + y) * 2 + r // 2 % 2) * 2 + r % 2 for z, y in order]
        for r in range(NR)
    ]


def column_exchange(x):
    return lax.all_to_all(x, AXES, 0, 0, axis_index_groups=column_groups(), tiled=True)


def swap(x, axes):
    size = 2 ** len(axes)
    return lax.ppermute(x, axes, [(i, size - 1 - i) for i in range(size)])


CHIPS = (("xh",), ("xl",), ("xl", "xh"))


def per_device(points, lengthscale, targets):
    own, copies = pl.pallas_call(
        pack,
        in_specs=[pl.BlockSpec(memory_space=pltpu.HBM)] * 3,
        out_specs=[pl.BlockSpec(memory_space=VMEM)] * 2,
        out_shape=[shape(1, 16, OWN), shape(NC, 16, OWN)],
        scratch_shapes=[
            pltpu.VMEM((8, OWN), f32),
            pltpu.SMEM((8,), f32),
            pltpu.VMEM((8, OWN), f32),
            pltpu.SemaphoreType.DMA((3,)),
        ],
        compiler_params=pltpu.CompilerParams(vmem_limit_bytes=4 << 20),
        name="pack",
    )(*[pltpu.with_memory_space_constraint(a, pltpu.HBM) for a in (points, lengthscale, targets)])
    cols = column_exchange(copies)
    rows = jnp.concatenate([own, swap(own, ("core",))], 0)
    rows = jnp.concatenate([rows] + [swap(rows, axes) for axes in CHIPS], 0)
    kernel, part = call(
        first_product,
        [VMEM((NJ, NI), f32), shape(2, 4, 16, OWN)],
        "first_product",
        [rows, cols],
        vmem=24 << 20,
    )
    part = part[0] + swap(part[1], ("core",))
    parts = [part[0:1]] + [swap(part[k : k + 1], axes) for k, axes in enumerate(CHIPS, 1)]
    message, image = call(
        first_image, [shape(NC * 9, 1, OWN), shape(8, OWN)], "first_image", parts + [rows]
    )
    image_cols = column_exchange(message)
    kernel = pltpu.with_memory_space_constraint(kernel, VMEM)
    part, scalars = call(
        second_product,
        [shape(NR * 8 + 16, OWN), shape(8, OWN)],
        "second_product",
        [cols, image_cols, image, kernel],
        vmem=8 << 20,
    )
    part = call(
        core_sum, [shape(NR * 8 + 24, OWN)], "core_sum", [part, swap(part, ("core",))]
    )[0]
    parts = [part] + [swap(part, axes) for axes in CHIPS]
    keep, message = call(
        second_image,
        [shape(4, 8, OWN), shape(NC, 1, OWN)],
        "second_image",
        parts + [rows, scalars],
        scratch=[pltpu.VMEM((3, NR, 8, OWN), f32), pltpu.VMEM((4, NR * 8 + 24, OWN), f32)],
    )
    sums = column_exchange(message)
    residual, direction = call(
        finish, [shape(8, OWN), shape(8, OWN)], "finish", [keep, sums]
    )
    return residual, direction


def solution(mesh):
    fine = Mesh(mesh.devices.reshape(SIZES), AXES)
    placed = (P(None, AXES), P(), P(None, AXES))
    return jax.shard_map(
        per_device,
        mesh=fine,
        in_specs=placed,
        out_specs=(P(None, AXES), P(None, AXES)),
        check_vma=False,
    )
```

```python
import math

import jax
import jax.numpy as jnp
from jax import lax
from jax.experimental import pallas as pl
from jax.experimental.pallas import tpu as pltpu
from jax.sharding import Mesh
from jax.sharding import PartitionSpec as P

f32 = jnp.float32
bf16 = jnp.bfloat16
VMEM = pltpu.VMEM

AXES = ("z", "xl", "y", "xh", "core")
SIZES = (8, 2, 4, 2, 2)
NR, NC = 8, 32
OWN = 128
NI, NJ = NR * OWN, NC * OWN
NEAR = 2 * OWN
noise_level = 0.5

LOG2E = math.log2(math.e)
POINT_SCALE = math.sqrt(5.0) * LOG2E
SHIFT = 1.5 * LOG2E
REST = SHIFT * SHIFT / 3.0
FACTOR = 2.0**SHIFT * 0.75 / (SHIFT * SHIFT)

TI, TJ = 256, 256


def pieces(x):
    first = x.astype(bf16).astype(f32)
    rest = x - first
    second = rest.astype(bf16).astype(f32)
    return first, second, rest - second


def features(x, left):
    x = x * POINT_SCALE
    square = jnp.sum(x * x, axis=0, keepdims=True)
    a, b, c = pieces(x)
    s1, s2, s3 = pieces(square)
    one, zero = jnp.ones_like(square), jnp.zeros_like(square)
    if left:
        tail = [s1, s2, s3, one, one, one, zero, zero]
        parts = [a, a, b, b, a, c]
    else:
        tail = [one, one, one, s1, s2, s3, zero, zero]
        parts = [-2.0 * a, -2.0 * b, -2.0 * a, -2.0 * b, -2.0 * c, -2.0 * a]
    return jnp.concatenate(parts + [jnp.concatenate(tail, 0), jnp.zeros_like(a)], 0)


def matern(square):
    square = jnp.maximum(square, 1e-30)
    u = -SHIFT - square * lax.rsqrt(square)
    return (u * u + REST) * jnp.exp2(u)


def product(values, tile):
    high = tile.astype(bf16)
    low = (tile - high.astype(f32)).astype(bf16)
    out = jnp.dot(values, high, preferred_element_type=f32)
    return out + jnp.dot(values, low, preferred_element_type=f32)


def stacked(values):
    return jnp.concatenate(pieces(values), 0).astype(bf16)


def lanes(ref, first_row, count, start=0):
    return jnp.concatenate(
        [ref[start + k, first_row : first_row + 8, :] for k in range(count)], 1
    )


def total(x):
    return jnp.sum(x, axis=1, keepdims=True)


def pack(points_hbm, lengthscale_hbm, targets_hbm, own_ref, copies_ref, points_ref, lengthscale_ref, targets_ref, sems):
    arriving = [
        pltpu.make_async_copy(points_hbm, points_ref, sems.at[0]),
        pltpu.make_async_copy(lengthscale_hbm, lengthscale_ref, sems.at[1]),
        pltpu.make_async_copy(targets_hbm, targets_ref, sems.at[2]),
    ]
    for copy in arriving:
        copy.start()
    for copy in arriving:
        copy.wait()
    row = lax.broadcasted_iota(jnp.int32, (8, OWN), 0)
    scale = jnp.zeros((8, OWN), f32)
    for k in range(8):
        scale = jnp.where(row == k, lengthscale_ref[k], scale)
    scaled = points_ref[...] / scale
    targets = targets_ref[...]
    own_ref[0, 0:8, :] = scaled
    own_ref[0, 8:16, :] = targets
    for copy in range(NC):
        copies_ref[copy, 0:8, :] = scaled
        copies_ref[copy, 8:16, :] = targets


def my_row_block():
    return lax.axis_index("xl") * 4 + lax.axis_index("xh") * 2 + lax.axis_index("core")


def first_rows(points, right, values, kernel_ref):
    left = features(points, True).astype(bf16)
    out = []
    for i in range(0, points.shape[1], TI):
        acc = jnp.zeros((24, TI), f32)
        for j in range(0, NJ, TJ):
            square = jnp.dot(right[j : j + TJ], left[:, i : i + TI], preferred_element_type=f32)
            kernel_ref[j : j + TJ, i : i + TI] = matern(square)
            if j > 0:
                last = kernel_ref[j - TJ : j, i : i + TI]
                acc = acc + product(values[:, j - TJ : j], last)
        acc = acc + product(values[:, NJ - TJ :], kernel_ref[NJ - TJ :, i : i + TI])
        out.append((acc[0:8] + acc[8:16] + acc[16:24]) * FACTOR)
    return jnp.concatenate(out, 1)


def near_product(near_ref, cols_ref, kernel_ref, right_ref, part_ref, form_ref):
    right = features(lanes(cols_ref, 0, NC), False).T.astype(bf16)
    right_ref[...] = right
    values = stacked(lanes(cols_ref, 8, NC))
    part = first_rows(lanes(near_ref, 0, 2), right, values, kernel_ref)
    part_ref[0] = part[:, :OWN]
    part_ref[1] = part[:, OWN:]
    form_ref[...] = part[:, :OWN] * near_ref[0, 8:16, :] + part[:, OWN:] * near_ref[1, 8:16, :]


def far_product(xh_ref, xl_ref, both_ref, cols_ref, right_ref, near_part_ref, form_ref, kernel_ref, out_ref):
    refs = (xh_ref, xl_ref, both_ref)
    values = stacked(lanes(cols_ref, 8, NC))
    points = jnp.concatenate([lanes(ref, 0, 2) for ref in refs], 1)
    part = first_rows(points, right_ref, values, kernel_ref)
    form = form_ref[...]
    for core in range(2):
        out_ref[core, 0, 0:8, :] = near_part_ref[core]
        for chip, ref in enumerate(refs):
            first = (chip * 2 + core) * OWN
            block = part[:, first : first + OWN]
            out_ref[core, chip + 1, 0:8, :] = block
            form = form + block * ref[core, 8:16, :]
    form = jnp.broadcast_to(total(form), (8, OWN))
    for core in range(2):
        for chip in range(4):
            out_ref[core, chip, 8:16, :] = form


def at_lanes(columns):
    lane = lax.broadcasted_iota(jnp.int32, (8, OWN), 1)
    out = jnp.zeros((8, OWN), f32)
    for k, column in enumerate(columns):
        out = jnp.where(lane == k, column, out)
    return out


def first_image(own_ref, xh_ref, xl_ref, both_ref, rows_ref, out_ref, image_ref):
    sums = (own_ref[0] + xh_ref[0]) + (xl_ref[0] + both_ref[0])
    targets = rows_ref[0, 8:16, :]
    bb = jnp.zeros((8, OWN), f32)
    for k in range(NR):
        bb = bb + rows_ref[k, 8:16, :] * rows_ref[k, 8:16, :]
    bb = total(bb)
    image = sums[0:8] + noise_level * targets
    scalars = in_one_row([bb, sums[8:16, 0:1] + noise_level * bb])
    for copy in range(NC):
        for row in range(8):
            out_ref[9 * copy + row] = image[row : row + 1]
        out_ref[9 * copy + 8] = scalars
    image_ref[...] = image


def second_product(cols_ref, image_cols_ref, image_ref, near_ref, far_ref, out_ref, scalar_ref):
    sums = image_cols_ref[8]
    for k in range(1, NC):
        sums = sums + image_cols_ref[9 * k + 8]
    norm = column_of(sums, 0)
    step = norm / column_of(sums, 1)
    images = [image_cols_ref[9 * k : 9 * k + 8].reshape(8, OWN) for k in range(NC)]
    residual = lanes(cols_ref, 8, NC) - step * jnp.concatenate(images, 1)
    norm_part = jnp.broadcast_to(total(residual * residual), (8, OWN))
    values = stacked(residual)
    mine = my_row_block()
    for i in range(0, NI, TI):
        acc = jnp.zeros((24, TI), f32)
        kernel_ref, first = (near_ref, i) if i < NEAR else (far_ref, i - NEAR)
        for j in range(0, NJ, TJ):
            acc = acc + product(values[:, j : j + TJ], kernel_ref[j : j + TJ, first : first + TI])
        acc = (acc[0:8] + acc[8:16] + acc[16:24]) * FACTOR
        for k in range(TI // OWN):
            row = pl.multiple_of((mine ^ (i // OWN + k)) * 8, 8)
            out_ref[pl.ds(row, 8), :] = acc[:, k * OWN : (k + 1) * OWN]
    out_ref[NR * 8 : NR * 8 + 8, :] = norm_part
    out_ref[NR * 8 + 8 :, :] = image_ref[...]
    scalar_ref[...] = at_lanes([norm, step])


def core_sum(ours_ref, theirs_ref, out_ref):
    core = lax.axis_index("core")
    sums = NR * 8 + 8
    out_ref[0:sums, :] = ours_ref[0:sums, :] + theirs_ref[0:sums, :]
    out_ref[pl.ds(pl.multiple_of(sums + core * 8, 8), 8), :] = ours_ref[sums:, :]
    out_ref[pl.ds(pl.multiple_of(sums + 8 - core * 8, 8), 8), :] = theirs_ref[sums:, :]


def second_image(own_part, xh_part, xl_part, both_part, rows_ref, scalar_ref, own_ref, out_ref, keep_ref, part_ref):
    mine = my_row_block()
    chip = mine // 2
    for k, ref in enumerate((own_part, xh_part, xl_part, both_part)):
        part_ref[chip ^ k] = ref[...]
    norm, step = scalar_ref[:, 0:1], scalar_ref[:, 1:2]

    def summed(row):
        out = part_ref[0, row : row + 8, :]
        for k in range(1, 4):
            out = out + part_ref[k, row : row + 8, :]
        return out

    norm_next = summed(NR * 8)
    ratio = norm_next / norm
    residuals, images = [], []
    di = jnp.zeros((8, OWN), f32)
    ri = jnp.zeros((8, OWN), f32)
    ii = jnp.zeros((8, OWN), f32)
    for k in range(NR):
        target = rows_ref[mine ^ k, 8:16, :]
        first = NR * 8 + 8 + (k % 2) * 8
        image0 = part_ref[k // 2, first : first + 8, :]
        residual = target - step * image0
        direction = residual + ratio * target
        image = (summed(8 * k) + noise_level * residual) + ratio * image0
        keep_ref[0, k] = residual
        keep_ref[1, k] = direction
        keep_ref[2, k] = image
        residuals.append(residual)
        images.append(image)
        di = di + direction * image
        ri = ri + residual * image
        ii = ii + image * image
    ii = total(ii)
    guess = total(ri) / jnp.where(ii > 0.0, ii, 1.0)
    ss = jnp.zeros((8, OWN), f32)
    si = jnp.zeros((8, OWN), f32)
    for k in range(NR):
        left = residuals[k] - guess * images[k]
        ss = ss + left * left
        si = si + left * images[k]
    scalars = in_one_row([total(di), guess, total(ss), total(si), ii])
    for copy in range(NC):
        out_ref[copy] = scalars
    own_ref[0] = keep_ref[0, mine]
    own_ref[1] = keep_ref[1, mine]
    own_ref[2] = keep_ref[2, mine]
    own_ref[3] = norm_next


def in_one_row(columns):
    lane = lax.broadcasted_iota(jnp.int32, (8, OWN), 1)
    row = lax.broadcasted_iota(jnp.int32, (8, OWN), 0)
    out = jnp.zeros((8, OWN), f32)
    for k, column in enumerate(columns):
        out = jnp.where(lane == 8 * k + row, column, out)
    return jnp.sum(out, axis=0, keepdims=True)


def column_of(row_vector, k):
    lane = lax.broadcasted_iota(jnp.int32, (8, OWN), 1)
    row = lax.broadcasted_iota(jnp.int32, (8, OWN), 0)
    return total(jnp.where(lane == 8 * k + row, row_vector, 0.0))


def finish(own_ref, sums_ref, residual_ref, direction_ref):
    norm = own_ref[3][:, 0:1]
    rows = [sums_ref[k] for k in range(NC)]
    step = norm / column_of(sum(rows[1:], rows[0]), 0)
    norm_next = jnp.zeros((8, 1), f32)
    for k in range(NC):
        guess, ss, si, ii = [column_of(rows[k], q) for q in range(1, 5)]
        off = step - guess
        norm_next = norm_next + (ss + off * (off * ii - 2.0 * si))
    residual = own_ref[0] - step * own_ref[2]
    residual_ref[...] = residual
    direction_ref[...] = residual + (norm_next / norm) * own_ref[1]


def call(kernel, outs, name, args, scratch=(), vmem=4 << 20, cost=None):
    return pl.pallas_call(
        kernel,
        in_specs=[
            pl.BlockSpec(memory_space=VMEM) for _ in args
        ],
        out_specs=[pl.BlockSpec(memory_space=VMEM)] * len(outs),
        out_shape=outs,
        scratch_shapes=scratch,
        compiler_params=pltpu.CompilerParams(vmem_limit_bytes=vmem),
        cost_estimate=cost,
        name=name,
    )(*args)


def shape(*dims):
    return jax.ShapeDtypeStruct(dims, f32)


def column_groups():
    order = [
        ((z + 4) % 8, ((y if z % 2 == 0 else 3 - y) + 2) % 4) for z in range(8) for y in range(4)
    ]
    return [
        [(((z * 2 + r // 4) * 4 + y) * 2 + r // 2 % 2) * 2 + r % 2 for z, y in order]
        for r in range(NR)
    ]


def column_exchange(x):
    return lax.all_to_all(x, AXES, 0, 0, axis_index_groups=column_groups(), tiled=True)


def swap(x, axes):
    size = 2 ** len(axes)
    return lax.ppermute(x, axes, [(i, size - 1 - i) for i in range(size)])


CHIPS = (("xh",), ("xl",), ("xl", "xh"))


def per_device(points, lengthscale, targets):
    own, copies = pl.pallas_call(
        pack,
        in_specs=[pl.BlockSpec(memory_space=pltpu.HBM)] * 3,
        out_specs=[pl.BlockSpec(memory_space=VMEM)] * 2,
        out_shape=[shape(1, 16, OWN), shape(NC, 16, OWN)],
        scratch_shapes=[
            pltpu.VMEM((8, OWN), f32),
            pltpu.SMEM((8,), f32),
            pltpu.VMEM((8, OWN), f32),
            pltpu.SemaphoreType.DMA((3,)),
        ],
        compiler_params=pltpu.CompilerParams(vmem_limit_bytes=4 << 20),
        name="pack",
    )(*[pltpu.with_memory_space_constraint(a, pltpu.HBM) for a in (points, lengthscale, targets)])
    cols = column_exchange(copies)
    near = jnp.concatenate([own, swap(own, ("core",))], 0)
    far = [swap(near, axes) for axes in CHIPS]
    near_kernel, right, near_part, form = call(
        near_product,
        [VMEM((NJ, NEAR), f32), jax.ShapeDtypeStruct((NJ, 64), bf16), shape(2, 8, OWN), shape(8, OWN)],
        "near_product",
        [near, cols],
        vmem=16 << 20,
        cost=pl.CostEstimate(flops=2 * NJ * NEAR * 128, bytes_accessed=4 * NJ * NEAR, transcendentals=2 * NJ * NEAR),
    )
    far_kernel, part = call(
        far_product,
        [VMEM((NJ, NI - NEAR), f32), shape(2, 4, 16, OWN)],
        "far_product",
        far + [cols, right, near_part, form],
        vmem=20 << 20,
    )
    rows = jnp.concatenate([near] + far, 0)
    part = part[0] + swap(part[1], ("core",))
    parts = [part[0:1]] + [swap(part[k : k + 1], axes) for k, axes in enumerate(CHIPS, 1)]
    message, image = call(
        first_image, [shape(NC * 9, 1, OWN), shape(8, OWN)], "first_image", parts + [rows]
    )
    image_cols = column_exchange(message)
    near_kernel = pltpu.with_memory_space_constraint(near_kernel, VMEM)
    far_kernel = pltpu.with_memory_space_constraint(far_kernel, VMEM)
    part, scalars = call(
        second_product,
        [shape(NR * 8 + 16, OWN), shape(8, OWN)],
        "second_product",
        [cols, image_cols, image, near_kernel, far_kernel],
        vmem=8 << 20,
    )
    part = call(
        core_sum, [shape(NR * 8 + 24, OWN)], "core_sum", [part, swap(part, ("core",))]
    )[0]
    parts = [part] + [swap(part, axes) for axes in CHIPS]
    keep, message = call(
        second_image,
        [shape(4, 8, OWN), shape(NC, 1, OWN)],
        "second_image",
        parts + [rows, scalars],
        scratch=[pltpu.VMEM((3, NR, 8, OWN), f32), pltpu.VMEM((4, NR * 8 + 24, OWN), f32)],
    )
    sums = column_exchange(message)
    residual, direction = call(
        finish, [shape(8, OWN), shape(8, OWN)], "finish", [keep, sums]
    )
    return residual, direction


def solution(mesh):
    fine = Mesh(mesh.devices.reshape(SIZES), AXES)
    placed = (P(None, AXES), P(), P(None, AXES))
    return jax.shard_map(
        per_device,
        mesh=fine,
        in_specs=placed,
        out_specs=(P(None, AXES), P(None, AXES)),
        check_vma=False,
    )
```

```python
import math

import jax
import jax.numpy as jnp
from jax import lax
from jax.experimental import pallas as pl
from jax.experimental.pallas import tpu as pltpu
from jax.sharding import Mesh
from jax.sharding import PartitionSpec as P

f32 = jnp.float32
bf16 = jnp.bfloat16
VMEM = pltpu.VMEM

AXES = ("z", "xl", "y", "xh", "core")
SIZES = (8, 2, 4, 2, 2)
NR, NC = 8, 32
OWN = 128
NI, NJ = NR * OWN, NC * OWN
NEAR = 2 * OWN
noise_level = 0.5

LOG2E = math.log2(math.e)
POINT_SCALE = math.sqrt(5.0) * LOG2E
SHIFT = 1.5 * LOG2E
REST = SHIFT * SHIFT / 3.0
FACTOR = 2.0**SHIFT * 0.75 / (SHIFT * SHIFT)

TI, TJ = 256, 256


def pieces(x):
    first = x.astype(bf16).astype(f32)
    rest = x - first
    second = rest.astype(bf16).astype(f32)
    return first, second, rest - second


def features(x, left):
    x = x * POINT_SCALE
    square = jnp.sum(x * x, axis=0, keepdims=True)
    a, b, c = pieces(x)
    s1, s2, s3 = pieces(square)
    one, zero = jnp.ones_like(square), jnp.zeros_like(square)
    if left:
        tail = [s1, s2, s3, one, one, one, zero, zero]
        parts = [a, a, b, b, a, c]
    else:
        tail = [one, one, one, s1, s2, s3, zero, zero]
        parts = [-2.0 * a, -2.0 * b, -2.0 * a, -2.0 * b, -2.0 * c, -2.0 * a]
    return jnp.concatenate(parts + [jnp.concatenate(tail, 0), jnp.zeros_like(a)], 0)


def matern(square):
    square = jnp.maximum(square, 1e-30)
    u = -SHIFT - square * lax.rsqrt(square)
    return (u * u + REST) * jnp.exp2(u)


def product(values, tile):
    high = tile.astype(bf16)
    low = (tile - high.astype(f32)).astype(bf16)
    out = jnp.dot(values, high, preferred_element_type=f32)
    return out + jnp.dot(values, low, preferred_element_type=f32)


def stacked(values):
    return jnp.concatenate(pieces(values), 0).astype(bf16)


def lanes(ref, first_row, count, start=0):
    return jnp.concatenate(
        [ref[start + k, first_row : first_row + 8, :] for k in range(count)], 1
    )


def total(x):
    return jnp.sum(x, axis=1, keepdims=True)


def pack(points_hbm, targets_hbm, own_ref, copies_ref, sems):
    points = pltpu.make_async_copy(points_hbm, own_ref.at[0, 0:8, :], sems.at[0])
    targets = pltpu.make_async_copy(targets_hbm, own_ref.at[0, 8:16, :], sems.at[1])
    points.start()
    targets.start()
    points.wait()
    targets.wait()
    for copy in range(NC):
        copies_ref[copy] = own_ref[0]


def near_points(near_ref, lengthscale_hbm, near_out_ref, scale_ref, lengthscale_ref, sem):
    copy = pltpu.make_async_copy(lengthscale_hbm, lengthscale_ref, sem)
    copy.start()
    copy.wait()
    row = lax.broadcasted_iota(jnp.int32, (8, OWN), 0)
    scale = jnp.zeros((8, OWN), f32)
    for k in range(8):
        scale = jnp.where(row == k, lengthscale_ref[k], scale)
    scale_ref[...] = scale
    for block in range(2):
        near_out_ref[block, 0:8, :] = near_ref[block, 0:8, :] / scale
        near_out_ref[block, 8:16, :] = near_ref[block, 8:16, :]


def my_row_block():
    return lax.axis_index("xl") * 4 + lax.axis_index("xh") * 2 + lax.axis_index("core")


def first_rows(points, right, values, kernel_ref):
    left = features(points, True).astype(bf16)
    out = []
    for i in range(0, points.shape[1], TI):
        acc = jnp.zeros((24, TI), f32)
        for j in range(0, NJ, TJ):
            square = jnp.dot(right[j : j + TJ], left[:, i : i + TI], preferred_element_type=f32)
            kernel_ref[j : j + TJ, i : i + TI] = matern(square)
            if j > 0:
                last = kernel_ref[j - TJ : j, i : i + TI]
                acc = acc + product(values[:, j - TJ : j], last)
        acc = acc + product(values[:, NJ - TJ :], kernel_ref[NJ - TJ :, i : i + TI])
        out.append((acc[0:8] + acc[8:16] + acc[16:24]) * FACTOR)
    return jnp.concatenate(out, 1)


def near_product(near_ref, cols_ref, scale_ref, kernel_ref, right_ref, part_ref, form_ref):
    right = features(lanes(cols_ref, 0, NC) / scale_ref[:, 0:1], False).T.astype(bf16)
    right_ref[...] = right
    values = stacked(lanes(cols_ref, 8, NC))
    part = first_rows(lanes(near_ref, 0, 2), right, values, kernel_ref)
    part_ref[0] = part[:, :OWN]
    part_ref[1] = part[:, OWN:]
    form_ref[...] = part[:, :OWN] * near_ref[0, 8:16, :] + part[:, OWN:] * near_ref[1, 8:16, :]


def far_product(xh_ref, xl_ref, both_ref, cols_ref, scale_ref, right_ref, near_part_ref, form_ref, kernel_ref, out_ref):
    refs = (xh_ref, xl_ref, both_ref)
    values = stacked(lanes(cols_ref, 8, NC))
    points = jnp.concatenate([lanes(ref, 0, 2) for ref in refs], 1)
    part = first_rows(points / scale_ref[:, 0:1], right_ref, values, kernel_ref)
    form = form_ref[...]
    for core in range(2):
        out_ref[core, 0, 0:8, :] = near_part_ref[core]
        for chip, ref in enumerate(refs):
            first = (chip * 2 + core) * OWN
            block = part[:, first : first + OWN]
            out_ref[core, chip + 1, 0:8, :] = block
            form = form + block * ref[core, 8:16, :]
    form = jnp.broadcast_to(total(form), (8, OWN))
    for core in range(2):
        for chip in range(4):
            out_ref[core, chip, 8:16, :] = form


def at_lanes(columns):
    lane = lax.broadcasted_iota(jnp.int32, (8, OWN), 1)
    out = jnp.zeros((8, OWN), f32)
    for k, column in enumerate(columns):
        out = jnp.where(lane == k, column, out)
    return out


def first_image(own_ref, both_ref, xl_ref, xh_ref, rows_ref, out_ref, image_ref):
    sums = (own_ref[0] + xh_ref[0]) + (xl_ref[0] + both_ref[0])
    targets = rows_ref[0, 8:16, :]
    bb = jnp.zeros((8, OWN), f32)
    for k in range(NR):
        bb = bb + rows_ref[k, 8:16, :] * rows_ref[k, 8:16, :]
    bb = total(bb)
    image = sums[0:8] + noise_level * targets
    scalars = in_one_row([bb, sums[8:16, 0:1] + noise_level * bb])
    for copy in range(NC):
        for row in range(8):
            out_ref[9 * copy + row] = image[row : row + 1]
        out_ref[9 * copy + 8] = scalars
    image_ref[...] = image


def second_product(cols_ref, image_cols_ref, image_ref, near_ref, far_ref, out_ref, scalar_ref):
    sums = image_cols_ref[8]
    for k in range(1, NC):
        sums = sums + image_cols_ref[9 * k + 8]
    norm = column_of(sums, 0)
    step = norm / column_of(sums, 1)
    images = [image_cols_ref[9 * k : 9 * k + 8].reshape(8, OWN) for k in range(NC)]
    residual = lanes(cols_ref, 8, NC) - step * jnp.concatenate(images, 1)
    norm_part = jnp.broadcast_to(total(residual * residual), (8, OWN))
    values = stacked(residual)
    mine = my_row_block()
    for i in range(0, NI, TI):
        acc = jnp.zeros((24, TI), f32)
        kernel_ref, first = (near_ref, i) if i < NEAR else (far_ref, i - NEAR)
        for j in range(0, NJ, TJ):
            acc = acc + product(values[:, j : j + TJ], kernel_ref[j : j + TJ, first : first + TI])
        acc = (acc[0:8] + acc[8:16] + acc[16:24]) * FACTOR
        for k in range(TI // OWN):
            row = pl.multiple_of((mine ^ (i // OWN + k)) * 8, 8)
            out_ref[pl.ds(row, 8), :] = acc[:, k * OWN : (k + 1) * OWN]
    out_ref[NR * 8 : NR * 8 + 8, :] = norm_part
    out_ref[NR * 8 + 8 :, :] = image_ref[...]
    scalar_ref[...] = at_lanes([norm, step])


def core_sum(ours_ref, theirs_ref, out_ref):
    core = lax.axis_index("core")
    sums = NR * 8 + 8
    out_ref[0:sums, :] = ours_ref[0:sums, :] + theirs_ref[0:sums, :]
    out_ref[pl.ds(pl.multiple_of(sums + core * 8, 8), 8), :] = ours_ref[sums:, :]
    out_ref[pl.ds(pl.multiple_of(sums + 8 - core * 8, 8), 8), :] = theirs_ref[sums:, :]


def second_image(own_part, both_part, xl_part, xh_part, rows_ref, scalar_ref, own_ref, out_ref, keep_ref, part_ref):
    mine = my_row_block()
    chip = mine // 2
    for k, ref in enumerate((own_part, xh_part, xl_part, both_part)):
        part_ref[chip ^ k] = ref[...]
    norm, step = scalar_ref[:, 0:1], scalar_ref[:, 1:2]

    def summed(row):
        out = part_ref[0, row : row + 8, :]
        for k in range(1, 4):
            out = out + part_ref[k, row : row + 8, :]
        return out

    norm_next = summed(NR * 8)
    ratio = norm_next / norm
    residuals, images = [], []
    di = jnp.zeros((8, OWN), f32)
    ri = jnp.zeros((8, OWN), f32)
    ii = jnp.zeros((8, OWN), f32)
    for k in range(NR):
        target = rows_ref[mine ^ k, 8:16, :]
        first = NR * 8 + 8 + (k % 2) * 8
        image0 = part_ref[k // 2, first : first + 8, :]
        residual = target - step * image0
        direction = residual + ratio * target
        image = (summed(8 * k) + noise_level * residual) + ratio * image0
        keep_ref[0, k] = residual
        keep_ref[1, k] = direction
        keep_ref[2, k] = image
        residuals.append(residual)
        images.append(image)
        di = di + direction * image
        ri = ri + residual * image
        ii = ii + image * image
    ii = total(ii)
    guess = total(ri) / jnp.where(ii > 0.0, ii, 1.0)
    ss = jnp.zeros((8, OWN), f32)
    si = jnp.zeros((8, OWN), f32)
    for k in range(NR):
        left = residuals[k] - guess * images[k]
        ss = ss + left * left
        si = si + left * images[k]
    scalars = in_one_row([total(di), guess, total(ss), total(si), ii])
    for copy in range(NC):
        out_ref[copy] = scalars
    own_ref[0] = keep_ref[0, mine]
    own_ref[1] = keep_ref[1, mine]
    own_ref[2] = keep_ref[2, mine]
    own_ref[3] = norm_next


def in_one_row(columns):
    lane = lax.broadcasted_iota(jnp.int32, (8, OWN), 1)
    row = lax.broadcasted_iota(jnp.int32, (8, OWN), 0)
    out = jnp.zeros((8, OWN), f32)
    for k, column in enumerate(columns):
        out = jnp.where(lane == 8 * k + row, column, out)
    return jnp.sum(out, axis=0, keepdims=True)


def column_of(row_vector, k):
    lane = lax.broadcasted_iota(jnp.int32, (8, OWN), 1)
    row = lax.broadcasted_iota(jnp.int32, (8, OWN), 0)
    return total(jnp.where(lane == 8 * k + row, row_vector, 0.0))


def finish(own_ref, sums_ref, residual_ref, direction_ref):
    norm = own_ref[3][:, 0:1]
    rows = [sums_ref[k] for k in range(NC)]
    step = norm / column_of(sum(rows[1:], rows[0]), 0)
    norm_next = jnp.zeros((8, 1), f32)
    for k in range(NC):
        guess, ss, si, ii = [column_of(rows[k], q) for q in range(1, 5)]
        off = step - guess
        norm_next = norm_next + (ss + off * (off * ii - 2.0 * si))
    residual = own_ref[0] - step * own_ref[2]
    residual_ref[...] = residual
    direction_ref[...] = residual + (norm_next / norm) * own_ref[1]


def call(kernel, outs, name, args, scratch=(), vmem=4 << 20, cost=None):
    return pl.pallas_call(
        kernel,
        in_specs=[
            pl.BlockSpec(memory_space=VMEM) for _ in args
        ],
        out_specs=[pl.BlockSpec(memory_space=VMEM)] * len(outs),
        out_shape=outs,
        scratch_shapes=scratch,
        compiler_params=pltpu.CompilerParams(vmem_limit_bytes=vmem),
        cost_estimate=cost,
        name=name,
    )(*args)


def shape(*dims):
    return jax.ShapeDtypeStruct(dims, f32)


def column_groups():
    order = [
        ((z + 4) % 8, ((y if z % 2 == 0 else 3 - y) + 2) % 4) for z in range(8) for y in range(4)
    ]
    return [
        [(((z * 2 + r // 4) * 4 + y) * 2 + r // 2 % 2) * 2 + r % 2 for z, y in order]
        for r in range(NR)
    ]


def column_exchange(x):
    return lax.all_to_all(x, AXES, 0, 0, axis_index_groups=column_groups(), tiled=True)


def swap(x, axes):
    size = 2 ** len(axes)
    return lax.ppermute(x, axes, [(i, size - 1 - i) for i in range(size)])


CHIPS = (("xh",), ("xl",), ("xl", "xh"))


def per_device(points, lengthscale, targets):
    own, copies = pl.pallas_call(
        pack,
        in_specs=[pl.BlockSpec(memory_space=pltpu.HBM)] * 2,
        out_specs=[pl.BlockSpec(memory_space=VMEM)] * 2,
        out_shape=[shape(1, 16, OWN), VMEM((NC, 16, OWN), f32)],
        scratch_shapes=[pltpu.SemaphoreType.DMA((2,))],
        compiler_params=pltpu.CompilerParams(vmem_limit_bytes=4 << 20),
        name="pack",
    )(*[pltpu.with_memory_space_constraint(a, pltpu.HBM) for a in (points, targets)])
    cols = column_exchange(copies)
    near = jnp.concatenate([own, swap(own, ("core",))], 0)
    far = [swap(near, axes) for axes in CHIPS]
    scaled_near, scale = pl.pallas_call(
        near_points,
        in_specs=[pl.BlockSpec(memory_space=VMEM), pl.BlockSpec(memory_space=pltpu.HBM)],
        out_specs=[pl.BlockSpec(memory_space=VMEM)] * 2,
        out_shape=[shape(2, 16, OWN), shape(8, OWN)],
        scratch_shapes=[pltpu.SMEM((8,), f32), pltpu.SemaphoreType.DMA],
        compiler_params=pltpu.CompilerParams(vmem_limit_bytes=4 << 20),
        name="near_points",
    )(near, pltpu.with_memory_space_constraint(lengthscale, pltpu.HBM))
    near_kernel, right, near_part, form = call(
        near_product,
        [VMEM((NJ, NEAR), f32), jax.ShapeDtypeStruct((NJ, 64), bf16), shape(2, 8, OWN), shape(8, OWN)],
        "near_product",
        [scaled_near, cols, scale],
        vmem=16 << 20,
        cost=pl.CostEstimate(flops=2 * NJ * NEAR * 128, bytes_accessed=4 * NJ * NEAR, transcendentals=2 * NJ * NEAR),
    )
    far_kernel, part = call(
        far_product,
        [VMEM((NJ, NI - NEAR), f32), shape(2, 4, 16, OWN)],
        "far_product",
        far + [cols, scale, right, near_part, form],
        vmem=20 << 20,
    )
    rows = jnp.concatenate([near] + far, 0)
    part = part[0] + swap(part[1], ("core",))
    parts = [part[0:1]] + [swap(part[k : k + 1], axes) for k, axes in enumerate(CHIPS, 1)]
    message, image = call(
        first_image, [shape(NC * 9, 1, OWN), shape(8, OWN)], "first_image", parts[:1] + parts[:0:-1] + [rows]
    )
    image_cols = column_exchange(message)
    near_kernel = pltpu.with_memory_space_constraint(near_kernel, VMEM)
    far_kernel = pltpu.with_memory_space_constraint(far_kernel, VMEM)
    part, scalars = call(
        second_product,
        [shape(NR * 8 + 16, OWN), shape(8, OWN)],
        "second_product",
        [cols, image_cols, image, near_kernel, far_kernel],
        vmem=8 << 20,
    )
    part = call(
        core_sum, [shape(NR * 8 + 24, OWN)], "core_sum", [part, swap(part, ("core",))]
    )[0]
    parts = [part] + [swap(part, axes) for axes in CHIPS]
    keep, message = call(
        second_image,
        [shape(4, 8, OWN), shape(NC, 1, OWN)],
        "second_image",
        parts[:1] + parts[:0:-1] + [rows, scalars],
        scratch=[pltpu.VMEM((3, NR, 8, OWN), f32), pltpu.VMEM((4, NR * 8 + 24, OWN), f32)],
    )
    sums = column_exchange(message)
    residual, direction = call(
        finish, [shape(8, OWN), shape(8, OWN)], "finish", [keep, sums]
    )
    return residual, direction


def solution(mesh):
    fine = Mesh(mesh.devices.reshape(SIZES), AXES)
    placed = (P(None, AXES), P(), P(None, AXES))
    return jax.shard_map(
        per_device,
        mesh=fine,
        in_specs=placed,
        out_specs=(P(None, AXES), P(None, AXES)),
        check_vma=False,
    )
```

```python
import math

import jax
import jax.numpy as jnp
from jax import lax
from jax.experimental import pallas as pl
from jax.experimental.pallas import tpu as pltpu
from jax.sharding import Mesh
from jax.sharding import PartitionSpec as P

f32 = jnp.float32
bf16 = jnp.bfloat16
VMEM = pltpu.VMEM

AXES = ("z", "xl", "y", "xh", "core")
SIZES = (8, 2, 4, 2, 2)
NR, NC = 8, 32
OWN = 128
NI, NJ = NR * OWN, NC * OWN
NEAR = 2 * OWN
noise_level = 0.5

LOG2E = math.log2(math.e)
POINT_SCALE = math.sqrt(5.0) * LOG2E
SHIFT = 1.5 * LOG2E
REST = SHIFT * SHIFT / 3.0
FACTOR = 2.0**SHIFT * 0.75 / (SHIFT * SHIFT)

TI, TJ = 256, 256


def pieces(x):
    first = x.astype(bf16).astype(f32)
    rest = x - first
    second = rest.astype(bf16).astype(f32)
    return first, second, rest - second


def features(x, left):
    x = x * POINT_SCALE
    square = jnp.sum(x * x, axis=0, keepdims=True)
    a, b, c = pieces(x)
    s1, s2, s3 = pieces(square)
    one, zero = jnp.ones_like(square), jnp.zeros_like(square)
    if left:
        tail = [s1, s2, s3, one, one, one, zero, zero]
        parts = [a, a, b, b, a, c]
    else:
        tail = [one, one, one, s1, s2, s3, zero, zero]
        parts = [-2.0 * a, -2.0 * b, -2.0 * a, -2.0 * b, -2.0 * c, -2.0 * a]
    return jnp.concatenate(parts + [jnp.concatenate(tail, 0), jnp.zeros_like(a)], 0)


def matern(square):
    square = jnp.maximum(square, 1e-30)
    u = -SHIFT - square * lax.rsqrt(square)
    return (u * u + REST) * jnp.exp2(u)


def product(values, tile):
    high = tile.astype(bf16)
    low = (tile - high.astype(f32)).astype(bf16)
    out = jnp.dot(values, high, preferred_element_type=f32)
    return out + jnp.dot(values, low, preferred_element_type=f32)


def stacked(values):
    return jnp.concatenate(pieces(values), 0).astype(bf16)


def lanes(ref, first_row, count, start=0):
    return jnp.concatenate(
        [ref[start + k, first_row : first_row + 8, :] for k in range(count)], 1
    )


def total(x):
    return jnp.sum(x, axis=1, keepdims=True)


def pack(points_hbm, targets_hbm, own_ref, copies_ref, sems):
    points = pltpu.make_async_copy(points_hbm, own_ref.at[0, 0:8, :], sems.at[0])
    targets = pltpu.make_async_copy(targets_hbm, own_ref.at[0, 8:16, :], sems.at[1])
    points.start()
    targets.start()
    points.wait()
    targets.wait()
    for copy in range(NC):
        copies_ref[copy] = own_ref[0]


def near_points(near_ref, lengthscale_hbm, near_out_ref, scale_ref, lengthscale_ref, sem):
    copy = pltpu.make_async_copy(lengthscale_hbm, lengthscale_ref, sem)
    copy.start()
    copy.wait()
    row = lax.broadcasted_iota(jnp.int32, (8, OWN), 0)
    scale = jnp.zeros((8, OWN), f32)
    for k in range(8):
        scale = jnp.where(row == k, lengthscale_ref[k], scale)
    scale_ref[...] = scale
    for block in range(2):
        near_out_ref[block, 0:8, :] = near_ref[block, 0:8, :] / scale
        near_out_ref[block, 8:16, :] = near_ref[block, 8:16, :]


def my_row_block():
    return lax.axis_index("xl") * 4 + lax.axis_index("xh") * 2 + lax.axis_index("core")


def first_rows(points, right, values, kernel_ref):
    left = features(points, True).astype(bf16)
    out = []
    for i in range(0, points.shape[1], TI):
        acc = jnp.zeros((24, TI), f32)
        for j in range(0, NJ, TJ):
            square = jnp.dot(right[j : j + TJ], left[:, i : i + TI], preferred_element_type=f32)
            kernel_ref[j : j + TJ, i : i + TI] = matern(square)
            if j > 0:
                last = kernel_ref[j - TJ : j, i : i + TI]
                acc = acc + product(values[:, j - TJ : j], last)
        acc = acc + product(values[:, NJ - TJ :], kernel_ref[NJ - TJ :, i : i + TI])
        out.append((acc[0:8] + acc[8:16] + acc[16:24]) * FACTOR)
    return jnp.concatenate(out, 1)


def near_product(near_ref, cols_ref, scale_ref, kernel_ref, right_ref, part_ref, form_ref):
    right = features(lanes(cols_ref, 0, NC) / scale_ref[:, 0:1], False).T.astype(bf16)
    right_ref[...] = right
    values = stacked(lanes(cols_ref, 8, NC))
    part = first_rows(lanes(near_ref, 0, 2), right, values, kernel_ref)
    part_ref[0] = part[:, :OWN]
    part_ref[1] = part[:, OWN:]
    form_ref[...] = part[:, :OWN] * near_ref[0, 8:16, :] + part[:, OWN:] * near_ref[1, 8:16, :]


def far_product(xh_ref, xl_ref, both_ref, cols_ref, scale_ref, right_ref, near_part_ref, form_ref, kernel_ref, out_ref):
    refs = (xh_ref, xl_ref, both_ref)
    values = stacked(lanes(cols_ref, 8, NC))
    points = jnp.concatenate([lanes(ref, 0, 2) for ref in refs], 1)
    part = first_rows(points / scale_ref[:, 0:1], right_ref, values, kernel_ref)
    form = form_ref[...]
    for core in range(2):
        out_ref[core, 0, 0:8, :] = near_part_ref[core]
        for chip, ref in enumerate(refs):
            first = (chip * 2 + core) * OWN
            block = part[:, first : first + OWN]
            out_ref[core, chip + 1, 0:8, :] = block
            form = form + block * ref[core, 8:16, :]
    form = jnp.broadcast_to(total(form), (8, OWN))
    for core in range(2):
        for chip in range(4):
            out_ref[core, chip, 8:16, :] = form


def at_lanes(columns):
    lane = lax.broadcasted_iota(jnp.int32, (8, OWN), 1)
    out = jnp.zeros((8, OWN), f32)
    for k, column in enumerate(columns):
        out = jnp.where(lane == k, column, out)
    return out


def first_image(own_ref, both_ref, xl_ref, xh_ref, rows_ref, out_ref, image_ref):
    sums = (own_ref[0] + xh_ref[0]) + (xl_ref[0] + both_ref[0])
    targets = rows_ref[0, 8:16, :]
    bb = jnp.zeros((8, OWN), f32)
    for k in range(NR):
        bb = bb + rows_ref[k, 8:16, :] * rows_ref[k, 8:16, :]
    bb = total(bb)
    image = sums[0:8] + noise_level * targets
    scalars = in_one_row([bb, sums[8:16, 0:1] + noise_level * bb])
    for copy in range(NC):
        for row in range(8):
            out_ref[9 * copy + row] = image[row : row + 1]
        out_ref[9 * copy + 8] = scalars
    image_ref[...] = image


def second_product(cols_ref, image_cols_ref, image_ref, near_ref, far_ref, out_ref, scalar_ref):
    sums = image_cols_ref[8]
    for k in range(1, NC):
        sums = sums + image_cols_ref[9 * k + 8]
    norm = column_of(sums, 0)
    step = norm / column_of(sums, 1)
    images = [image_cols_ref[9 * k : 9 * k + 8].reshape(8, OWN) for k in range(NC)]
    residual = lanes(cols_ref, 8, NC) - step * jnp.concatenate(images, 1)
    norm_part = jnp.broadcast_to(total(residual * residual), (8, OWN))
    values = stacked(residual)
    mine = my_row_block()
    for i in range(0, NI, TI):
        acc = jnp.zeros((24, TI), f32)
        kernel_ref, first = (near_ref, i) if i < NEAR else (far_ref, i - NEAR)
        for j in range(0, NJ, 2 * TJ):
            tile = kernel_ref[j : j + 2 * TJ, first : first + TI]
            acc = acc + product(values[:, j : j + 2 * TJ], tile)
        acc = (acc[0:8] + acc[8:16] + acc[16:24]) * FACTOR
        for k in range(TI // OWN):
            row = pl.multiple_of((mine ^ (i // OWN + k)) * 8, 8)
            out_ref[pl.ds(row, 8), :] = acc[:, k * OWN : (k + 1) * OWN]
    out_ref[NR * 8 : NR * 8 + 8, :] = norm_part
    out_ref[NR * 8 + 8 :, :] = image_ref[...]
    scalar_ref[...] = at_lanes([norm, step])


def core_sum(ours_ref, theirs_ref, out_ref):
    core = lax.axis_index("core")
    sums = NR * 8 + 8
    out_ref[0:sums, :] = ours_ref[0:sums, :] + theirs_ref[0:sums, :]
    out_ref[pl.ds(pl.multiple_of(sums + core * 8, 8), 8), :] = ours_ref[sums:, :]
    out_ref[pl.ds(pl.multiple_of(sums + 8 - core * 8, 8), 8), :] = theirs_ref[sums:, :]


def second_image(own_part, both_part, xl_part, xh_part, rows_ref, scalar_ref, own_ref, out_ref, keep_ref, part_ref):
    mine = my_row_block()
    chip = mine // 2
    for k, ref in enumerate((own_part, xh_part, xl_part, both_part)):
        part_ref[chip ^ k] = ref[...]
    norm, step = scalar_ref[:, 0:1], scalar_ref[:, 1:2]

    def summed(row):
        out = part_ref[0, row : row + 8, :]
        for k in range(1, 4):
            out = out + part_ref[k, row : row + 8, :]
        return out

    norm_next = summed(NR * 8)
    ratio = norm_next / norm
    residuals, images = [], []
    di = jnp.zeros((8, OWN), f32)
    ri = jnp.zeros((8, OWN), f32)
    ii = jnp.zeros((8, OWN), f32)
    for k in range(NR):
        target = rows_ref[mine ^ k, 8:16, :]
        first = NR * 8 + 8 + (k % 2) * 8
        image0 = part_ref[k // 2, first : first + 8, :]
        residual = target - step * image0
        direction = residual + ratio * target
        image = (summed(8 * k) + noise_level * residual) + ratio * image0
        keep_ref[0, k] = residual
        keep_ref[1, k] = direction
        keep_ref[2, k] = image
        residuals.append(residual)
        images.append(image)
        di = di + direction * image
        ri = ri + residual * image
        ii = ii + image * image
    ii = total(ii)
    guess = total(ri) / jnp.where(ii > 0.0, ii, 1.0)
    ss = jnp.zeros((8, OWN), f32)
    si = jnp.zeros((8, OWN), f32)
    for k in range(NR):
        left = residuals[k] - guess * images[k]
        ss = ss + left * left
        si = si + left * images[k]
    scalars = in_one_row([total(di), guess, total(ss), total(si), ii])
    for copy in range(NC):
        out_ref[copy] = scalars
    own_ref[0] = keep_ref[0, mine]
    own_ref[1] = keep_ref[1, mine]
    own_ref[2] = keep_ref[2, mine]
    own_ref[3] = norm_next


def in_one_row(columns):
    lane = lax.broadcasted_iota(jnp.int32, (8, OWN), 1)
    row = lax.broadcasted_iota(jnp.int32, (8, OWN), 0)
    out = jnp.zeros((8, OWN), f32)
    for k, column in enumerate(columns):
        out = jnp.where(lane == 8 * k + row, column, out)
    return jnp.sum(out, axis=0, keepdims=True)


def column_of(row_vector, k):
    lane = lax.broadcasted_iota(jnp.int32, (8, OWN), 1)
    row = lax.broadcasted_iota(jnp.int32, (8, OWN), 0)
    return total(jnp.where(lane == 8 * k + row, row_vector, 0.0))


def finish(own_ref, sums_ref, residual_ref, direction_ref):
    norm = own_ref[3][:, 0:1]
    rows = [sums_ref[k] for k in range(NC)]
    step = norm / column_of(sum(rows[1:], rows[0]), 0)
    norm_next = jnp.zeros((8, 1), f32)
    for k in range(NC):
        guess, ss, si, ii = [column_of(rows[k], q) for q in range(1, 5)]
        off = step - guess
        norm_next = norm_next + (ss + off * (off * ii - 2.0 * si))
    residual = own_ref[0] - step * own_ref[2]
    residual_ref[...] = residual
    direction_ref[...] = residual + (norm_next / norm) * own_ref[1]


def call(kernel, outs, name, args, scratch=(), vmem=4 << 20, cost=None):
    return pl.pallas_call(
        kernel,
        in_specs=[
            pl.BlockSpec(memory_space=VMEM) for _ in args
        ],
        out_specs=[pl.BlockSpec(memory_space=VMEM)] * len(outs),
        out_shape=outs,
        scratch_shapes=scratch,
        compiler_params=pltpu.CompilerParams(vmem_limit_bytes=vmem),
        cost_estimate=cost,
        name=name,
    )(*args)


def shape(*dims):
    return jax.ShapeDtypeStruct(dims, f32)


def column_groups():
    order = [
        ((z + 4) % 8, ((y if z % 2 == 0 else 3 - y) + 2) % 4) for z in range(8) for y in range(4)
    ]
    return [
        [(((z * 2 + r // 4) * 4 + y) * 2 + r // 2 % 2) * 2 + r % 2 for z, y in order]
        for r in range(NR)
    ]


def column_exchange(x):
    return lax.all_to_all(x, AXES, 0, 0, axis_index_groups=column_groups(), tiled=True)


def swap(x, axes):
    size = 2 ** len(axes)
    return lax.ppermute(x, axes, [(i, size - 1 - i) for i in range(size)])


CHIPS = (("xh",), ("xl",), ("xl", "xh"))


def per_device(points, lengthscale, targets):
    own, copies = pl.pallas_call(
        pack,
        in_specs=[pl.BlockSpec(memory_space=pltpu.HBM)] * 2,
        out_specs=[pl.BlockSpec(memory_space=VMEM)] * 2,
        out_shape=[shape(1, 16, OWN), VMEM((NC, 16, OWN), f32)],
        scratch_shapes=[pltpu.SemaphoreType.DMA((2,))],
        compiler_params=pltpu.CompilerParams(vmem_limit_bytes=4 << 20),
        name="pack",
    )(*[pltpu.with_memory_space_constraint(a, pltpu.HBM) for a in (points, targets)])
    cols = column_exchange(copies)
    near = jnp.concatenate([own, swap(own, ("core",))], 0)
    far = [swap(near, axes) for axes in CHIPS]
    scaled_near, scale = pl.pallas_call(
        near_points,
        in_specs=[pl.BlockSpec(memory_space=VMEM), pl.BlockSpec(memory_space=pltpu.HBM)],
        out_specs=[pl.BlockSpec(memory_space=VMEM)] * 2,
        out_shape=[shape(2, 16, OWN), shape(8, OWN)],
        scratch_shapes=[pltpu.SMEM((8,), f32), pltpu.SemaphoreType.DMA],
        compiler_params=pltpu.CompilerParams(vmem_limit_bytes=4 << 20),
        name="near_points",
    )(near, pltpu.with_memory_space_constraint(lengthscale, pltpu.HBM))
    near_kernel, right, near_part, form = call(
        near_product,
        [VMEM((NJ, NEAR), f32), jax.ShapeDtypeStruct((NJ, 64), bf16), shape(2, 8, OWN), shape(8, OWN)],
        "near_product",
        [scaled_near, cols, scale],
        vmem=16 << 20,
        cost=pl.CostEstimate(flops=2 * NJ * NEAR * 128, bytes_accessed=4 * NJ * NEAR, transcendentals=2 * NJ * NEAR),
    )
    far_kernel, part = call(
        far_product,
        [VMEM((NJ, NI - NEAR), f32), shape(2, 4, 16, OWN)],
        "far_product",
        far + [cols, scale, right, near_part, form],
        vmem=20 << 20,
    )
    rows = jnp.concatenate([near] + far, 0)
    part = part[0] + swap(part[1], ("core",))
    parts = [part[0:1]] + [swap(part[k : k + 1], axes) for k, axes in enumerate(CHIPS, 1)]
    message, image = call(
        first_image, [shape(NC * 9, 1, OWN), shape(8, OWN)], "first_image", parts[:1] + parts[:0:-1] + [rows]
    )
    image_cols = column_exchange(message)
    near_kernel = pltpu.with_memory_space_constraint(near_kernel, VMEM)
    far_kernel = pltpu.with_memory_space_constraint(far_kernel, VMEM)
    part, scalars = call(
        second_product,
        [shape(NR * 8 + 16, OWN), shape(8, OWN)],
        "second_product",
        [cols, image_cols, image, near_kernel, far_kernel],
        vmem=8 << 20,
    )
    part = call(
        core_sum, [shape(NR * 8 + 24, OWN)], "core_sum", [part, swap(part, ("core",))]
    )[0]
    parts = [part] + [swap(part, axes) for axes in CHIPS]
    keep, message = call(
        second_image,
        [shape(4, 8, OWN), shape(NC, 1, OWN)],
        "second_image",
        parts[:1] + parts[:0:-1] + [rows, scalars],
        scratch=[pltpu.VMEM((3, NR, 8, OWN), f32), pltpu.VMEM((4, NR * 8 + 24, OWN), f32)],
    )
    sums = column_exchange(message)
    residual, direction = call(
        finish, [shape(8, OWN), shape(8, OWN)], "finish", [keep, sums]
    )
    return residual, direction


def solution(mesh):
    fine = Mesh(mesh.devices.reshape(SIZES), AXES)
    placed = (P(None, AXES), P(), P(None, AXES))
    return jax.shard_map(
        per_device,
        mesh=fine,
        in_specs=placed,
        out_specs=(P(None, AXES), P(None, AXES)),
        check_vma=False,
    )
```
